32 devices in a mesh: row: 16 (over z, y, x), col: 2 (over core).
Axes of the slice: x: 2, y: 2, z: 4, core: 2. Of those that a mesh axis runs over, the one named last changes fastest.
Arguments:
- rhs: float32 [16, 2, 12, 192, 128], P('row', 'col'), may hold values from -6 to 6
- smoother: bfloat16 [16, 2, 3, 3, 768], P('row', 'col'), may hold values from -0.375 to 2.375
- blocks: bfloat16 [16, 2, 12, 192, 1536], P('row', 'col'), may hold values from -0.15625 to 0.15625
- col_index: int32 [16, 2, 12, 8], P('row', 'col'), may hold values from 0 to 27, as said below
- send_list: int32 [16, 2, 4, 4], P('row', 'col'), may hold values from 0 to 11, as said below
- agg_id: int32 [16, 2, 12], P('row', 'col'), may hold values from 0 to 3, as said below
- prolong: bfloat16 [16, 2, 6, 2304], P('row', 'col'), may hold values from -0.4375 to 0.4375
- coarse_inverse: bfloat16 [768, 768], P('row'), may hold values from -0.21875 to 0.21875
Outputs:
- smoothed_solution: float32 [16, 2, 12, 192, 128], P('row', 'col')
The draws below stay inside these ranges and needn't reach their ends.
Inputs may be any that keep to these rules, and one draw needn't show every extreme that they name: `col_index`: A value below 12 names a block row of the same device; the value 12 + 4 * g + j names slot j of ghost group g. Every ghost slot is named by some entry of each device. `send_list`: the 4 blocks of one device and group are distinct. `agg_id`: every aggregate of a device holds at least one block row.
All inputs are finite; a program needn't handle non-finite values.
Results may differ from the reference program's by a relative error of at most 0.0029.
Values may be sent and summed in bfloat16 or wider, within the bound.
A program may use at most 64 MiB of HBM per device.

```python
import math
import jax
import jax.numpy as jnp
from jax import lax

GR = 64
DOF = 192
K = 8
NB = 12
NRHS = 128
CD = 6
HB = 4
AGG_DEV = 4
NC = 768
N_ROW = 16
N_COL = 2


def distinct_ranks(key, leading, entries):
    scores = jax.random.randint(key, leading + (entries,), 0, 1 << 20, dtype=jnp.int32) * entries
    scores = scores + jnp.arange(entries, dtype=jnp.int32)
    ordering = jnp.argsort(scores, axis=-1).astype(jnp.int32)
    position = jnp.argsort(ordering, axis=-1).astype(jnp.int32)
    return (position, ordering)


def draw_smoother(key, part):
    key_spread = jax.random.fold_in(key, 1)
    key_diagonal = jax.random.fold_in(key, 2)
    full_shape = (N_ROW, N_COL, 3, 3, NB * GR)
    spread = jax.random.uniform(key_spread, full_shape, jnp.float32, -0.375, 0.375)
    diagonal = jnp.exp(jax.random.uniform(key_diagonal, full_shape, jnp.float32, math.log(0.5), math.log(2.0)))
    identity = (jnp.arange(3)[:, None] == jnp.arange(3)[None, :]).astype(jnp.float32)[None, None, :, :, None]
    return (spread + identity * diagonal).astype(jnp.bfloat16)


def draw_col_index(key, part):
    entries = NB * K
    ghost_slots = 4 * HB
    position, ordering = distinct_ranks(jax.random.fold_in(key, 11), (N_ROW, N_COL), entries)
    filler = jax.random.randint(jax.random.fold_in(key, 12), (N_ROW, N_COL, entries), 0, NB + ghost_slots, dtype=jnp.int32)
    values = jnp.where(position < ghost_slots, NB + position, filler)
    return values.reshape((N_ROW, N_COL, NB, K)).astype(jnp.int32)


def draw_send_list(key, part):
    position, ordering = distinct_ranks(jax.random.fold_in(key, 21), (N_ROW, N_COL, 4), NB)
    return ordering[:, :, :, :HB].astype(jnp.int32)


def draw_agg_id(key, part):
    position, ordering = distinct_ranks(jax.random.fold_in(key, 31), (N_ROW, N_COL), NB)
    filler = jax.random.randint(jax.random.fold_in(key, 32), (N_ROW, N_COL, NB), 0, AGG_DEV, dtype=jnp.int32)
    return jnp.where(position < AGG_DEV, position, filler).astype(jnp.int32)


def block_scale(stream_key, shape, shards, low, high):
    def one(axis_at, shards_of):
        steps = jax.random.uniform(jax.random.fold_in(jax.random.fold_in(stream_key, 6), axis_at), (shards_of,), jnp.float32, low / len(shards), high / len(shards))
        return jnp.repeat(jnp.exp(steps), shape[axis_at] // shards_of).reshape((-1,) + (1,) * (len(shape) - axis_at - 1))

    loudness = one(*shards[0])
    for cut in shards[1:]:
        loudness = loudness * one(*cut)
    return loudness


def bell_draw(key, shape, scale, limit, cuts=(), kind=jnp.bfloat16):
    gain = block_scale(key, shape, cuts, -0.22, 0.18) if cuts else 1.0
    drawn = jax.random.normal(key, shape, jnp.float32) * scale * gain
    return jnp.minimum(jnp.maximum(drawn, -limit), limit).astype(kind)


def setup_inputs(seed: int = 0) -> dict:
    keys = jax.random.split(jax.random.key(seed), 9)
    return {
        "rhs": bell_draw(keys[0], (N_ROW, N_COL, NB, DOF, NRHS), 1.0, 6.0, ((0, 16), (1, 2)), jnp.float32),
        "smoother": draw_smoother(jax.random.fold_in(keys[8], 71), 0),
        "blocks": bell_draw(keys[2], (N_ROW, N_COL, NB, DOF, K * DOF), (K * DOF) ** -0.5, 0.15625, ((0, 16), (1, 2))),
        "col_index": draw_col_index(jax.random.fold_in(keys[8], 71), 0),
        "send_list": draw_send_list(jax.random.fold_in(keys[8], 71), 0),
        "agg_id": draw_agg_id(jax.random.fold_in(keys[8], 71), 0),
        "prolong": bell_draw(keys[6], (N_ROW, N_COL, CD, NB * DOF), DOF ** -0.5, 0.4375, ((0, 16), (1, 2))),
        "coarse_inverse": bell_draw(keys[7], (NC, NC), NC ** -0.5, 0.21875, ((0, 16),)),
    }


damping = 0.6


def point_smooth(coefficients, vector):
    leading = vector.shape[:2]
    blocks = vector.shape[2]
    grains = vector.shape[3] // 3
    columns = vector.shape[4]
    factors = coefficients.astype(jnp.float32).reshape(leading + (3, 3, blocks, grains))
    pieces = vector.reshape(leading + (blocks, 3, grains, columns))
    outputs = []
    for component in range(3):
        summed = factors[:, :, component, 0, :, :, None] * pieces[:, :, :, 0]
        summed = summed + factors[:, :, component, 1, :, :, None] * pieces[:, :, :, 1]
        summed = summed + factors[:, :, component, 2, :, :, None] * pieces[:, :, :, 2]
        outputs.append(summed)
    return damping * jnp.stack(outputs, axis=3).reshape(vector.shape)


def ghost_sources(vector_low, send_list):
    stacked = [vector_low]
    moves = ((1, 0), (-1, 0), (1, 1), (-1, 1))
    for group in range(4):
        amount, along = moves[group]
        rolled_vector = jnp.roll(vector_low, amount, axis=along)
        rolled_list = jnp.roll(send_list[:, :, group], amount, axis=along)
        stacked.append(jnp.take_along_axis(rolled_vector, rolled_list[:, :, :, None, None], axis=2))
    return jnp.concatenate(stacked, axis=2)


def apply_operator(blocks, col_index, send_list, vector):
    vector_low = vector.astype(jnp.bfloat16)
    source = ghost_sources(vector_low, send_list)
    device_count = N_ROW * N_COL
    flat_blocks = blocks.reshape((device_count,) + blocks.shape[2:])
    flat_index = col_index.reshape((device_count,) + col_index.shape[2:])
    flat_source = source.reshape((device_count,) + source.shape[2:])

    def device_product(operands):
        matrix, columns, gathered = operands
        picked = jnp.take(gathered, columns.reshape(-1), axis=0)
        picked = picked.reshape((columns.shape[0], -1, gathered.shape[-1]))
        return jnp.einsum("nde,ner->ndr", matrix.astype(jnp.float32), picked.astype(jnp.float32),
                          precision=lax.Precision.HIGHEST)

    result = lax.map(device_product, (flat_blocks, flat_index, flat_source))
    return result.reshape(vector.shape)


def reference(rhs, smoother, blocks, col_index, send_list, agg_id, prolong, coarse_inverse):
    first_iter = point_smooth(smoother, rhs)
    residual_first = rhs - apply_operator(blocks, col_index, send_list, first_iter)
    update_second = point_smooth(smoother, residual_first)
    second_iter = first_iter + update_second
    residual_second = residual_first - apply_operator(blocks, col_index, send_list, update_second)
    shaped = prolong.astype(jnp.float32).reshape((N_ROW, N_COL, CD, NB, DOF))
    residual_low = lax.optimization_barrier(residual_second.astype(jnp.bfloat16))
    local_terms = jnp.einsum("abknd,abndr->abnkr", shaped, residual_low.astype(jnp.float32),
                             precision=lax.Precision.HIGHEST)
    onehot = (agg_id[:, :, None, :] == jnp.arange(AGG_DEV, dtype=jnp.int32)[None, None, :, None]).astype(jnp.float32)
    coarse_residual = jnp.einsum("abxn,abnkr->abxkr", onehot, local_terms, precision=lax.Precision.HIGHEST)
    coarse_rhs = coarse_residual.astype(jnp.bfloat16).reshape((NC, NRHS))
    coarse_solution = jnp.dot(coarse_inverse, coarse_rhs, preferred_element_type=jnp.float32)
    coarse_rounded = coarse_solution.astype(jnp.bfloat16).reshape((N_ROW, N_COL, AGG_DEV, CD, NRHS))
    coarse_rounded = lax.optimization_barrier(coarse_rounded)
    picked = jnp.take_along_axis(coarse_rounded, agg_id[:, :, :, None, None], axis=2)
    correction = jnp.einsum("abknd,abnkr->abndr", shaped, picked.astype(jnp.float32),
                            precision=lax.Precision.HIGHEST)
    after_coarse = second_iter + correction
    residual_third = residual_second - apply_operator(blocks, col_index, send_list, correction)
    return after_coarse + point_smooth(smoother, residual_third)
```

```python
import functools

import jax
import jax.numpy as jnp
from jax import lax
from jax.experimental import pallas as pl
from jax.experimental.pallas import tpu as pltpu
from jax.sharding import PartitionSpec as P

damping = 0.6
f32 = jnp.float32
bf16 = jnp.bfloat16
MESH = pl.DeviceIdType.MESH
UNROLL = 3


def iota(shape, axis):
    return lax.broadcasted_iota(jnp.int32, shape, axis)


def dot(a, b):
    return jnp.dot(a, b, preferred_element_type=f32)


def dot_first(a, b):
    return lax.dot_general(a, b, (((0,), (0,)), ((), ())), preferred_element_type=f32)


def ones_where(condition):
    return jnp.where(condition, 1.0, 0.0).astype(bf16)


def kernel(
    dims,
    rhs_hbm, smoother_ref, blocks_hbm, col_ref, send_ref, agg_ref, prolong_ref, cinv_ref,
    out_hbm,
    rhs, blocks, first, res, later, factors, small, wide,
    source1, source2, source3, packed1, packed2, pmsg, pghost, cinv32, crow, cghost, cstack,
    residual_low, pexpt, gathered, grhs, quick, out, local,
    load_sem, out_sem, h1_send, h1_recv, h2_send, h2_recv, p_send, p_recv, c_send, c_recv,
    ga_send, ga_recv, gb_send, gb_recv, gc_send, gc_recv,
):
    n_row, n_col, f1, f2, nb, dof, vec, kk, cd, agg, hb = dims
    gr = dof // 3
    cu = cd * agg
    row, col = lax.axis_index("row"), lax.axis_index("col")
    at1, at2 = row // f2, row % f2

    load_rhs = pltpu.make_async_copy(rhs_hbm.at[0, 0], rhs, load_sem.at[0])
    load_rhs.start()
    parts = 4
    load_blocks = [
        pltpu.make_async_copy(
            blocks_hbm.at[0, 0, pl.ds(p * (nb // parts), nb // parts)],
            blocks.at[pl.ds(p * (nb // parts), nb // parts)],
            load_sem.at[1 + p],
        )
        for p in range(parts)
    ]
    for load in load_blocks:
        load.start()

    row_up, row_down = (row + 1) % n_row, (row + n_row - 1) % n_row
    col_up, col_down = (col + 1) % n_col, (col + n_col - 1) % n_col
    targets = [(row_up, col), (row_down, col), (row, col_up), (row, col_down)]
    line_a = [((at1 + d) % f1 * f2 + at2, col) for d in range(1, f1)]
    line_b = [(at1 * f2 + (at2 + d) % f2, col) for d in range(1, f2)]
    line_c = [(row, (col + d) % n_col) for d in range(1, n_col)]
    greeted = targets + line_a + line_b + line_c
    barrier = pltpu.get_barrier_semaphore()
    for other in greeted:
        pl.semaphore_signal(barrier, inc=1, device_id=other, device_id_type=MESH)

    small[...] = jnp.zeros_like(small)
    for i in range(3):
        small[i * 3 : i * 3 + 3, :] = smoother_ref[0, 0, i].astype(f32)
    lanes = iota((16, 9 * vec), 1)
    starts = iota((16, 9 * vec), 0) * vec
    spread = dot_first(
        small[...].astype(bf16), ones_where((lanes >= starts) & (lanes < starts + vec))
    )
    for q in range(9):
        for n in range(nb):
            factors[q, n] = damping * spread[n * gr : (n + 1) * gr, q * vec : (q + 1) * vec]

    def smooth(n, value):
        v = [value[j * gr : (j + 1) * gr] for j in range(3)]
        return jnp.concatenate(
            [
                factors[3 * i, n] * v[0]
                + factors[3 * i + 1, n] * v[1]
                + factors[3 * i + 2, n] * v[2]
                for i in range(3)
            ],
            axis=0,
        )

    def loop(low, high, body):
        def several(step, carry):
            for u in range(UNROLL):
                body(low + step * UNROLL + u)
            return carry

        lax.fori_loop(0, (high - low) // UNROLL, several, 0)

    def multiply(n, source):
        picked = jnp.concatenate([source[col_ref[0, 0, n, k]] for k in range(kk)], axis=0)
        return dot(blocks[n], picked)

    def halo(packed, source, send_sem, recv_sem):
        return [
            pltpu.make_async_remote_copy(
                src_ref=packed.at[g],
                dst_ref=source.at[pl.ds(nb + g * hb, hb)],
                send_sem=send_sem.at[g],
                recv_sem=recv_sem.at[g],
                device_id=targets[g],
                device_id_type=MESH,
            )
            for g in range(4)
        ]

    def pack(packed):
        for g in range(4):
            for j in range(hb):
                packed[g, j] = local[send_ref[0, 0, g, j]]

    load_rhs.wait()

    def first_body(n):
        value = smooth(n, rhs[n])
        first[n] = value
        source1[n] = value.astype(bf16)
        local[n] = value.astype(bf16)

    loop(0, nb, first_body)
    pack(packed1)
    pl.semaphore_wait(barrier, len(greeted))
    halo1 = halo(packed1, source1, h1_send, h1_recv)
    for copy in halo1:
        copy.start()

    wide[...] = jnp.zeros_like(wide)
    wide[0:cd, :] = prolong_ref[0, 0].astype(f32)
    rows, modes = iota((32, 8), 0), iota((32, 8), 1)
    hit = rows < 0
    for a in range(agg):
        hit = hit | ((rows == modes + a * cd) & (modes < cd))
    lane = iota((1, nb * dof), 1)
    owner = jnp.zeros((1, nb * dof), jnp.int32)
    for n in range(nb):
        owner = jnp.where(
            (lane >= n * dof) & (lane < (n + 1) * dof), agg_ref[0, 0, n] * cd, owner
        )
    owner = jnp.broadcast_to(owner, (32, nb * dof))
    unknown = iota((32, nb * dof), 0)
    expanded = dot(ones_where(hit), wide[...].astype(bf16))
    pexpt[...] = jnp.where(
        (unknown >= owner) & (unknown < owner + cd), expanded, 0.0
    ).astype(bf16)
    upright = dot_first(pexpt[...], ones_where(iota((32, vec), 0) == iota((32, vec), 1)))
    for n in range(nb):
        source3[n] = upright[n * dof : (n + 1) * dof].astype(bf16)
    origin, place = iota((vec, vec), 0), iota((vec, vec), 1)
    for g in range(4):
        total = jnp.zeros((dof, vec), f32)
        for j in range(hb):
            shift = ones_where((place == origin + j * cu) & (origin < cu))
            total = total + dot(source3[send_ref[0, 0, g, j]], shift)
        pmsg[g] = total.astype(bf16)

    cinv32[...] = cinv_ref[...].astype(f32)

    def coarse_rows(c):
        return cinv32[pl.ds(pl.multiple_of(c * cu, 8), cu), :]

    cstack[...] = jnp.zeros_like(cstack)
    cstack[0:cu] = coarse_rows(col)
    cstack[3 * cu : 4 * cu] = coarse_rows(col_down)
    cstack[4 * cu : 5 * cu] = coarse_rows(col_up)
    crow[...] = cstack[0:32].astype(bf16)

    for copy in halo1:
        copy.wait_recv()
    crow_copies = [
        pltpu.make_async_remote_copy(
            src_ref=crow,
            dst_ref=cghost.at[g],
            send_sem=c_send.at[g],
            recv_sem=c_recv.at[g],
            device_id=targets[g],
            device_id_type=MESH,
        )
        for g in range(2)
    ]
    for copy in crow_copies:
        copy.start()
    for load in load_blocks:
        load.wait()

    def second_body(n):
        value = rhs[n] - multiply(n, source1)
        res[n] = value
        update = smooth(n, value)
        later[n] = first[n] + update
        source2[n] = update.astype(bf16)
        local[n] = update.astype(bf16)

    loop(0, nb, second_body)
    pack(packed2)
    halo2 = halo(packed2, source2, h2_send, h2_recv)
    for copy in halo2:
        copy.start()

    for copy in crow_copies:
        copy.wait_recv()
    cstack[cu : 2 * cu] = cghost[0].astype(f32)[0:cu]
    cstack[2 * cu : 3 * cu] = cghost[1].astype(f32)[0:cu]

    for copy in halo2:
        copy.wait_recv()
    pmsg_copies = [
        pltpu.make_async_remote_copy(
            src_ref=pmsg.at[g],
            dst_ref=pghost.at[g],
            send_sem=p_send.at[g],
            recv_sem=p_recv.at[g],
            device_id=targets[g],
            device_id_type=MESH,
        )
        for g in range(4)
    ]
    for copy in pmsg_copies:
        copy.start()

    def third_body(n):
        value = res[n] - multiply(n, source2)
        res[n] = value
        residual_low[pl.ds(pl.multiple_of(n * dof, dof), dof), :] = value.astype(bf16)

    loop(0, nb, third_body)
    gathered[at1, at2, col] = dot(pexpt[...], residual_low[...]).astype(bf16)

    def step_copies(line, pick, mine, others, send_sem, recv_sem):
        sends, arrivals = [], []
        for d, target in enumerate(line):
            sends.append(
                pltpu.make_async_remote_copy(
                    src_ref=pick(mine),
                    dst_ref=pick(mine),
                    send_sem=send_sem.at[d],
                    recv_sem=recv_sem.at[d],
                    device_id=target,
                    device_id_type=MESH,
                )
            )
            arrivals.append(
                pltpu.make_async_remote_copy(
                    src_ref=pick(mine),
                    dst_ref=pick(others[d]),
                    send_sem=send_sem.at[d],
                    recv_sem=recv_sem.at[d],
                    device_id=target,
                    device_id_type=MESH,
                )
            )
        return sends, arrivals

    def behind(at, count):
        return [(at + count - d) % count for d in range(1, count)]

    a_sends, a_arrivals = step_copies(
        line_a, lambda i: gathered.at[i, at2, col], at1, behind(at1, f1), ga_send, ga_recv
    )
    b_sends, b_arrivals = step_copies(
        line_b, lambda i: gathered.at[:, i, col], at2, behind(at2, f2), gb_send, gb_recv
    )
    c_sends, c_arrivals = step_copies(
        line_c, lambda i: gathered.at[:, :, i], col, behind(col, n_col), gc_send, gc_recv
    )
    for copy in a_sends:
        copy.start()

    for copy in pmsg_copies:
        copy.wait_recv()
    for g in range(4):
        for j in range(hb):
            shift = ones_where(
                (place - (1 + g) * cu == origin - j * cu)
                & (origin >= j * cu)
                & (origin < (j + 1) * cu)
            )
            source3[nb + g * hb + j] = dot(pghost[g], shift).astype(bf16)

    def fourth_body(n):
        later[n] = later[n] + smooth(n, res[n])
        value = source3[n].astype(f32) - smooth(n, multiply(n, source3))
        high = value.astype(bf16)
        quick[n, :, 0:vec] = high
        quick[n, :, vec : 2 * vec] = (value - high.astype(f32)).astype(bf16)

    third = nb // 3 // UNROLL * UNROLL
    loop(0, third, fourth_body)
    for copy in a_arrivals:
        copy.wait_recv()
    for copy in b_sends:
        copy.start()
    loop(third, 2 * third, fourth_body)
    for copy in b_arrivals:
        copy.wait_recv()
    for copy in c_sends:
        copy.start()
    loop(2 * third, nb, fourth_body)
    for copy in c_arrivals:
        copy.wait_recv()

    def unpad(step, carry):
        for c in range(n_col):
            start = pl.multiple_of((step * n_col + c) * cu, 8)
            grhs[pl.ds(start, cu), :] = gathered[step // f2, step % f2, c].astype(f32)[0:cu]
        return carry

    lax.fori_loop(0, n_row, unpad, 0)
    coarse = dot(cstack[...].astype(bf16), grhs[...].astype(bf16)).astype(bf16)
    twice = jnp.concatenate([coarse, coarse], axis=0)
    out_copies = []
    for n in range(nb):
        out[n] = later[n] + dot(quick[n], twice)
        copy = pltpu.make_async_copy(out.at[n], out_hbm.at[0, 0, n], out_sem.at[n])
        copy.start()
        out_copies.append(copy)
    for copy in halo1 + crow_copies + halo2 + pmsg_copies + a_sends + b_sends + c_sends:
        copy.wait_send()
    for copy in out_copies:
        copy.wait()


def body(rhs, smoother, blocks, col_index, send_list, agg_id, prolong, coarse_inverse):
    n_row, n_col = lax.axis_size("row"), lax.axis_size("col")
    nb, dof, vec = rhs.shape[2:]
    kk = col_index.shape[3]
    hb = send_list.shape[3]
    cd = prolong.shape[2]
    nc = coarse_inverse.shape[1]
    agg = nc // (n_row * n_col) // cd
    cu = agg * cd
    f2 = 4 if n_row % 4 == 0 else 1
    f1 = n_row // f2
    dims = (n_row, n_col, f1, f2, nb, dof, vec, kk, cd, agg, hb)
    slots = nb + 4 * hb
    field = (nb, dof, vec)
    dma = pltpu.SemaphoreType.DMA
    vmem, smem, anywhere = (
        pl.BlockSpec(memory_space=pltpu.VMEM),
        pl.BlockSpec(memory_space=pltpu.SMEM),
        pl.BlockSpec(memory_space=pl.ANY),
    )
    return pl.pallas_call(
        functools.partial(kernel, dims),
        out_shape=jax.ShapeDtypeStruct(rhs.shape, f32),
        in_specs=[anywhere, vmem, anywhere, smem, smem, smem, vmem, vmem],
        out_specs=anywhere,
        scratch_shapes=[
            pltpu.VMEM(field, f32),
            pltpu.VMEM(blocks.shape[2:], bf16),
            pltpu.VMEM(field, f32),
            pltpu.VMEM(field, f32),
            pltpu.VMEM(field, f32),
            pltpu.VMEM((9, nb, dof // 3, vec), f32),
            pltpu.VMEM((16, nb * dof // 3), f32),
            pltpu.VMEM((8, nb * dof), f32),
            pltpu.VMEM((slots, dof, vec), bf16),
            pltpu.VMEM((slots, dof, vec), bf16),
            pltpu.VMEM((slots, dof, vec), bf16),
            pltpu.VMEM((4, hb, dof, vec), bf16),
            pltpu.VMEM((4, hb, dof, vec), bf16),
            pltpu.VMEM((4, dof, vec), bf16),
            pltpu.VMEM((4, dof, vec), bf16),
            pltpu.VMEM((n_col * cu, nc), f32),
            pltpu.VMEM((32, nc), bf16),
            pltpu.VMEM((2, 32, nc), bf16),
            pltpu.VMEM((vec, nc), f32),
            pltpu.VMEM((nb * dof, vec), bf16),
            pltpu.VMEM((32, nb * dof), bf16),
            pltpu.VMEM((f1, f2, n_col, 32, vec), bf16),
            pltpu.VMEM((nc, vec), f32),
            pltpu.VMEM((nb, dof, 2 * vec), bf16),
            pltpu.VMEM(field, f32),
            pltpu.VMEM(field, bf16),
            dma((5,)),
            dma((nb,)),
            dma((4,)),
            dma((4,)),
            dma((4,)),
            dma((4,)),
            dma((4,)),
            dma((4,)),
            dma((2,)),
            dma((2,)),
            dma((max(f1 - 1, 1),)),
            dma((max(f1 - 1, 1),)),
            dma((max(f2 - 1, 1),)),
            dma((max(f2 - 1, 1),)),
            dma((n_col - 1,)),
            dma((n_col - 1,)),
        ],
        compiler_params=pltpu.CompilerParams(
            collective_id=0, has_side_effects=True, vmem_limit_bytes=56 * 1024 * 1024
        ),
    )(rhs, smoother, blocks, col_index, send_list, agg_id, prolong, coarse_inverse)


def solution(mesh):
    placed = (
        P("row", "col", None, None, None),
        P("row", "col", None, None, None),
        P("row", "col", None, None, None),
        P("row", "col", None, None),
        P("row", "col", None, None),
        P("row", "col", None),
        P("row", "col", None, None),
        P("row", None),
    )
    return jax.shard_map(
        body,
        mesh=mesh,
        in_specs=placed,
        out_specs=P("row", "col", None, None, None),
        check_vma=False,
    )
```

```python
import functools

import jax
import jax.numpy as jnp
from jax import lax
from jax.experimental import pallas as pl
from jax.experimental.pallas import tpu as pltpu
from jax.sharding import PartitionSpec as P

damping = 0.6
f32 = jnp.float32
bf16 = jnp.bfloat16
MESH = pl.DeviceIdType.MESH
UNROLL = 6


def iota(shape, axis):
    return lax.broadcasted_iota(jnp.int32, shape, axis)


def dot(a, b):
    return jnp.dot(a, b, preferred_element_type=f32)


def dot_first(a, b):
    return lax.dot_general(a, b, (((0,), (0,)), ((), ())), preferred_element_type=f32)


def ones_where(condition):
    return jnp.where(condition, 1.0, 0.0).astype(bf16)


def kernel(
    dims,
    rhs_ref, smoother_ref, blocks_hbm, col_ref, send_ref, agg_ref, prolong_ref, cinv_ref,
    out_ref,
    blocks, first, res, later, factors, small, wide,
    source1, source2, source3, packed1, packed2, pmsg, pghost, cinv32, crow, cghost, cstack,
    residual_low, pexpt, gathered, grhs, quick, local,
    load_sem, h1_send, h1_recv, h2_send, h2_recv, p_send, p_recv, c_send, c_recv,
    ga_send, ga_recv, gb_send, gb_recv, gc_send, gc_recv,
):
    n_row, n_col, f1, f2, nb, dof, vec, kk, cd, agg, hb = dims
    gr = dof // 3
    cu = cd * agg
    row, col = lax.axis_index("row"), lax.axis_index("col")
    at1, at2 = row // f2, row % f2

    rhs = rhs_ref.at[0, 0]
    parts = 4
    load_blocks = [
        pltpu.make_async_copy(
            blocks_hbm.at[0, 0, pl.ds(p * (nb // parts), nb // parts)],
            blocks.at[pl.ds(p * (nb // parts), nb // parts)],
            load_sem.at[p],
        )
        for p in range(parts)
    ]
    for load in load_blocks:
        load.start()

    row_up, row_down = (row + 1) % n_row, (row + n_row - 1) % n_row
    col_up, col_down = (col + 1) % n_col, (col + n_col - 1) % n_col
    targets = [(row_up, col), (row_down, col), (row, col_up), (row, col_down)]
    line_a = [((at1 + d) % f1 * f2 + at2, col) for d in range(1, f1)]
    line_b = [(at1 * f2 + (at2 + d) % f2, col) for d in range(1, f2)]
    line_c = [(row, (col + d) % n_col) for d in range(1, n_col)]
    greeted = targets + line_a + line_b + line_c
    barrier = pltpu.get_barrier_semaphore()
    for other in greeted:
        pl.semaphore_signal(barrier, inc=1, device_id=other, device_id_type=MESH)

    small[...] = jnp.zeros_like(small)
    for i in range(3):
        small[i * 3 : i * 3 + 3, :] = smoother_ref[0, 0, i].astype(f32)
    lanes = iota((16, 9 * vec), 1)
    starts = iota((16, 9 * vec), 0) * vec
    spread = dot_first(
        small[...].astype(bf16), ones_where((lanes >= starts) & (lanes < starts + vec))
    )
    for q in range(9):
        for n in range(nb):
            factors[q, n] = damping * spread[n * gr : (n + 1) * gr, q * vec : (q + 1) * vec]

    def smooth(n, value):
        v = [value[j * gr : (j + 1) * gr] for j in range(3)]
        return jnp.concatenate(
            [
                factors[3 * i, n] * v[0]
                + factors[3 * i + 1, n] * v[1]
                + factors[3 * i + 2, n] * v[2]
                for i in range(3)
            ],
            axis=0,
        )

    def loop(low, high, body, unroll=UNROLL):
        def several(step, carry):
            for u in range(unroll):
                body(low + step * unroll + u)
            return carry

        lax.fori_loop(0, (high - low) // unroll, several, 0)

    def multiply(n, source):
        picked = jnp.concatenate([source[col_ref[0, 0, k, n]] for k in range(kk)], axis=0)
        return dot(blocks[n], picked)

    def halo(packed, source, send_sem, recv_sem):
        return [
            pltpu.make_async_remote_copy(
                src_ref=packed.at[g],
                dst_ref=source.at[pl.ds(nb + g * hb, hb)],
                send_sem=send_sem.at[g],
                recv_sem=recv_sem.at[g],
                device_id=targets[g],
                device_id_type=MESH,
            )
            for g in range(4)
        ]

    def pack(packed):
        for g in range(4):
            for j in range(hb):
                packed[g, j] = local[send_ref[0, 0, g, j]]

    def first_body(n):
        value = smooth(n, rhs[n])
        first[n] = value
        source1[n] = value.astype(bf16)

    halo1 = halo(packed1, source1, h1_send, h1_recv)
    for g in range(4):
        for j in range(hb):
            n = send_ref[0, 0, g, j]
            packed1[g, j] = smooth(n, rhs[n]).astype(bf16)
        if g == 0:
            pl.semaphore_wait(barrier, len(greeted))
        halo1[g].start()
    loop(0, nb, first_body)

    wide[...] = jnp.zeros_like(wide)
    wide[0:cd, :] = prolong_ref[0, 0].astype(f32)
    rows, modes = iota((32, 8), 0), iota((32, 8), 1)
    hit = rows < 0
    for a in range(agg):
        hit = hit | ((rows == modes + a * cd) & (modes < cd))
    lane = iota((1, nb * dof), 1)
    owner = jnp.zeros((1, nb * dof), jnp.int32)
    for n in range(nb):
        owner = jnp.where(
            (lane >= n * dof) & (lane < (n + 1) * dof), agg_ref[0, 0, n] * cd, owner
        )
    owner = jnp.broadcast_to(owner, (32, nb * dof))
    unknown = iota((32, nb * dof), 0)
    expanded = dot(ones_where(hit), wide[...].astype(bf16))
    pexpt[...] = jnp.where(
        (unknown >= owner) & (unknown < owner + cd), expanded, 0.0
    ).astype(bf16)
    upright = dot_first(pexpt[...], ones_where(iota((32, vec), 0) == iota((32, vec), 1)))
    for n in range(nb):
        source3[n] = upright[n * dof : (n + 1) * dof].astype(bf16)
    origin, place = iota((vec, vec), 0), iota((vec, vec), 1)
    for g in range(4):
        total = jnp.zeros((dof, vec), f32)
        for j in range(hb):
            shift = ones_where((place == origin + j * cu) & (origin < cu))
            total = total + dot(source3[send_ref[0, 0, g, j]], shift)
        pmsg[g] = total.astype(bf16)

    cinv32[...] = cinv_ref[...].astype(f32)

    def coarse_rows(c):
        return cinv32[pl.ds(pl.multiple_of(c * cu, 8), cu), :]

    cstack[...] = jnp.zeros_like(cstack)
    cstack[0:cu] = coarse_rows(col)
    cstack[3 * cu : 4 * cu] = coarse_rows(col_down)
    cstack[4 * cu : 5 * cu] = coarse_rows(col_up)
    crow[...] = cstack[0:32].astype(bf16)

    for copy in halo1:
        copy.wait_recv()
    crow_copies = [
        pltpu.make_async_remote_copy(
            src_ref=crow,
            dst_ref=cghost.at[g],
            send_sem=c_send.at[g],
            recv_sem=c_recv.at[g],
            device_id=targets[g],
            device_id_type=MESH,
        )
        for g in range(2)
    ]
    for copy in crow_copies:
        copy.start()
    pmsg_copies = [
        pltpu.make_async_remote_copy(
            src_ref=pmsg.at[g],
            dst_ref=pghost.at[g],
            send_sem=p_send.at[g],
            recv_sem=p_recv.at[g],
            device_id=targets[g],
            device_id_type=MESH,
        )
        for g in range(4)
    ]
    for copy in pmsg_copies:
        copy.start()

    for load in load_blocks:
        load.wait()

    def second_body(n):
        value = rhs[n] - multiply(n, source1)
        res[n] = value
        update = smooth(n, value)
        later[n] = first[n] + update
        source2[n] = update.astype(bf16)
        local[n] = update.astype(bf16)

    loop(0, nb, second_body)
    pack(packed2)
    halo2 = halo(packed2, source2, h2_send, h2_recv)
    for copy in halo2:
        copy.start()

    for copy in crow_copies:
        copy.wait_recv()
    cstack[cu : 2 * cu] = cghost[0].astype(f32)[0:cu]
    cstack[2 * cu : 3 * cu] = cghost[1].astype(f32)[0:cu]

    for copy in pmsg_copies:
        copy.wait_recv()
    for g in range(4):
        for j in range(hb):
            shift = ones_where(
                (place - (1 + g) * cu == origin - j * cu)
                & (origin >= j * cu)
                & (origin < (j + 1) * cu)
            )
            source3[nb + g * hb + j] = dot(pghost[g], shift).astype(bf16)

    def operator_body(n):
        value = source3[n].astype(f32) - smooth(n, multiply(n, source3))
        high = value.astype(bf16)
        quick[n, :, 0:vec] = high
        quick[n, :, vec : 2 * vec] = (value - high.astype(f32)).astype(bf16)

    loop(0, nb, operator_body)
    for copy in halo2:
        copy.wait_recv()
    def third_body(n):
        value = res[n] - multiply(n, source2)
        res[n] = value
        residual_low[pl.ds(pl.multiple_of(n * dof, dof), dof), :] = value.astype(bf16)

    loop(0, nb, third_body)
    gathered[at1, at2, col] = dot(pexpt[...], residual_low[...]).astype(bf16)

    def step_copies(line, pick, mine, others, send_sem, recv_sem):
        sends, arrivals = [], []
        for d, target in enumerate(line):
            sends.append(
                pltpu.make_async_remote_copy(
                    src_ref=pick(mine),
                    dst_ref=pick(mine),
                    send_sem=send_sem.at[d],
                    recv_sem=recv_sem.at[d],
                    device_id=target,
                    device_id_type=MESH,
                )
            )
            arrivals.append(
                pltpu.make_async_remote_copy(
                    src_ref=pick(mine),
                    dst_ref=pick(others[d]),
                    send_sem=send_sem.at[d],
                    recv_sem=recv_sem.at[d],
                    device_id=target,
                    device_id_type=MESH,
                )
            )
        return sends, arrivals

    def behind(at, count):
        return [(at + count - d) % count for d in range(1, count)]

    a_sends, a_arrivals = step_copies(
        line_a, lambda i: gathered.at[i, at2, col], at1, behind(at1, f1), ga_send, ga_recv
    )
    b_sends, b_arrivals = step_copies(
        line_b, lambda i: gathered.at[:, i, col], at2, behind(at2, f2), gb_send, gb_recv
    )
    c_sends, c_arrivals = step_copies(
        line_c, lambda i: gathered.at[:, :, i], col, behind(col, n_col), gc_send, gc_recv
    )
    for copy in a_sends:
        copy.start()

    def fourth_body(n):
        later[n] = later[n] + smooth(n, res[n])

    third = nb // 3 // 2 * 2
    loop(0, third, fourth_body, 2)
    for copy in a_arrivals:
        copy.wait_recv()
    for copy in b_sends:
        copy.start()
    loop(third, 2 * third, fourth_body, 2)
    for copy in b_arrivals:
        copy.wait_recv()
    for copy in c_sends:
        copy.start()
    loop(2 * third, nb, fourth_body, 2)
    for copy in c_arrivals:
        copy.wait_recv()

    def unpad(step, carry):
        for c in range(n_col):
            start = pl.multiple_of((step * n_col + c) * cu, 8)
            grhs[pl.ds(start, cu), :] = gathered[step // f2, step % f2, c].astype(f32)[0:cu]
        return carry

    lax.fori_loop(0, n_row, unpad, 0)
    coarse = dot(cstack[...].astype(bf16), grhs[...].astype(bf16)).astype(bf16)
    twice = jnp.concatenate([coarse, coarse], axis=0)
    for n in range(nb):
        out_ref[0, 0, n] = later[n] + dot(quick[n], twice)
    for copy in halo1 + crow_copies + halo2 + pmsg_copies + a_sends + b_sends + c_sends:
        copy.wait_send()


def body(rhs, smoother, blocks, col_index, send_list, agg_id, prolong, coarse_inverse):
    n_row, n_col = lax.axis_size("row"), lax.axis_size("col")
    nb, dof, vec = rhs.shape[2:]
    kk = col_index.shape[3]
    hb = send_list.shape[3]
    cd = prolong.shape[2]
    nc = coarse_inverse.shape[1]
    agg = nc // (n_row * n_col) // cd
    cu = agg * cd
    f2 = 4 if n_row % 4 == 0 else 1
    f1 = n_row // f2
    dims = (n_row, n_col, f1, f2, nb, dof, vec, kk, cd, agg, hb)
    slots = nb + 4 * hb
    field = (nb, dof, vec)
    dma = pltpu.SemaphoreType.DMA
    vmem, smem, anywhere = (
        pl.BlockSpec(memory_space=pltpu.VMEM),
        pl.BlockSpec(memory_space=pltpu.SMEM),
        pl.BlockSpec(memory_space=pl.ANY),
    )
    return pl.pallas_call(
        functools.partial(kernel, dims),
        out_shape=jax.ShapeDtypeStruct(rhs.shape, f32),
        in_specs=[vmem, vmem, anywhere, smem, smem, smem, vmem, vmem],
        out_specs=vmem,
        scratch_shapes=[
            pltpu.VMEM(blocks.shape[2:], bf16),
            pltpu.VMEM(field, f32),
            pltpu.VMEM(field, f32),
            pltpu.VMEM(field, f32),
            pltpu.VMEM((9, nb, dof // 3, vec), f32),
            pltpu.VMEM((16, nb * dof // 3), f32),
            pltpu.VMEM((8, nb * dof), f32),
            pltpu.VMEM((slots, dof, vec), bf16),
            pltpu.VMEM((slots, dof, vec), bf16),
            pltpu.VMEM((slots, dof, vec), bf16),
            pltpu.VMEM((4, hb, dof, vec), bf16),
            pltpu.VMEM((4, hb, dof, vec), bf16),
            pltpu.VMEM((4, dof, vec), bf16),
            pltpu.VMEM((4, dof, vec), bf16),
            pltpu.VMEM((n_col * cu, nc), f32),
            pltpu.VMEM((32, nc), bf16),
            pltpu.VMEM((2, 32, nc), bf16),
            pltpu.VMEM((vec, nc), f32),
            pltpu.VMEM((nb * dof, vec), bf16),
            pltpu.VMEM((32, nb * dof), bf16),
            pltpu.VMEM((f1, f2, n_col, 32, vec), bf16),
            pltpu.VMEM((nc, vec), f32),
            pltpu.VMEM((nb, dof, 2 * vec), bf16),
            pltpu.VMEM(field, bf16),
            dma((4,)),
            dma((4,)),
            dma((4,)),
            dma((4,)),
            dma((4,)),
            dma((4,)),
            dma((4,)),
            dma((2,)),
            dma((2,)),
            dma((max(f1 - 1, 1),)),
            dma((max(f1 - 1, 1),)),
            dma((max(f2 - 1, 1),)),
            dma((max(f2 - 1, 1),)),
            dma((n_col - 1,)),
            dma((n_col - 1,)),
        ],
        compiler_params=pltpu.CompilerParams(
            collective_id=0, has_side_effects=True, vmem_limit_bytes=48 * 1024 * 1024
        ),
    )(rhs, smoother, blocks, jnp.swapaxes(col_index, 2, 3), send_list, agg_id, prolong, coarse_inverse)


def solution(mesh):
    placed = (
        P("row", "col", None, None, None),
        P("row", "col", None, None, None),
        P("row", "col", None, None, None),
        P("row", "col", None, None),
        P("row", "col", None, None),
        P("row", "col", None),
        P("row", "col", None, None),
        P("row", None),
    )
    return jax.shard_map(
        body,
        mesh=mesh,
        in_specs=placed,
        out_specs=P("row", "col", None, None, None),
        check_vma=False,
    )
```

```python
import functools

import jax
import jax.numpy as jnp
from jax import lax
from jax.experimental import pallas as pl
from jax.experimental.pallas import tpu as pltpu
from jax.sharding import PartitionSpec as P

damping = 0.6
f32 = jnp.float32
bf16 = jnp.bfloat16
MESH = pl.DeviceIdType.MESH
UNROLL = 6


def iota(shape, axis):
    return lax.broadcasted_iota(jnp.int32, shape, axis)


def dot(a, b):
    return jnp.dot(a, b, preferred_element_type=f32)


def dot_first(a, b):
    return lax.dot_general(a, b, (((0,), (0,)), ((), ())), preferred_element_type=f32)


def ones_where(condition):
    return jnp.where(condition, 1.0, 0.0).astype(bf16)


def kernel(
    dims,
    rhs_hbm, smoother_hbm, blocks_hbm, col_hbm, send_hbm, agg_hbm, prolong_hbm, cinv_hbm,
    later_ref, quick_ref, twice_ref,
    rhs_ref, smoother_ref, col_ref, send_ref, agg_ref, prolong_ref, cinv_ref,
    blocks, first, res, later, factors, small, wide,
    source1, source2, source3, packed1, packed2, pmsg, pghost, cinv32, crow, cghost, cstack,
    residual_low, pexpt, gathered, grhs, quick, local,
    load_sem, out_sem, h1_send, h1_recv, h2_send, h2_recv, p_send, p_recv, c_send, c_recv,
    ga_send, ga_recv, gb_send, gb_recv, gc_send, gc_recv,
):
    n_row, n_col, f1, f2, nb, dof, vec, kk, cd, agg, hb = dims
    gr = dof // 3
    cu = cd * agg
    row, col = lax.axis_index("row"), lax.axis_index("col")
    at1, at2 = row // f2, row % f2

    loads = [
        pltpu.make_async_copy(source, target, load_sem.at[4 + at])
        for at, (source, target) in enumerate(
            [
                (smoother_hbm, smoother_ref),
                (rhs_hbm, rhs_ref),
                (send_hbm, send_ref),
                (col_hbm, col_ref),
                (agg_hbm, agg_ref),
                (prolong_hbm, prolong_ref),
                (cinv_hbm, cinv_ref),
            ]
        )
    ]
    for load in loads:
        load.start()
    rhs = rhs_ref.at[0, 0]
    parts = 4
    load_blocks = [
        pltpu.make_async_copy(
            blocks_hbm.at[0, 0, pl.ds(p * (nb // parts), nb // parts)],
            blocks.at[pl.ds(p * (nb // parts), nb // parts)],
            load_sem.at[p],
        )
        for p in range(parts)
    ]
    for load in load_blocks:
        load.start()

    row_up, row_down = (row + 1) % n_row, (row + n_row - 1) % n_row
    col_up, col_down = (col + 1) % n_col, (col + n_col - 1) % n_col
    targets = [(row_up, col), (row_down, col), (row, col_up), (row, col_down)]
    line_a = [((at1 + d) % f1 * f2 + at2, col) for d in range(1, f1)]
    line_b = [(at1 * f2 + (at2 + d) % f2, col) for d in range(1, f2)]
    line_c = [(row, (col + d) % n_col) for d in range(1, n_col)]
    greeted = targets + line_a + line_b + line_c
    barrier = pltpu.get_barrier_semaphore()
    for other in greeted:
        pl.semaphore_signal(barrier, inc=1, device_id=other, device_id_type=MESH)

    loads[0].wait()
    small[...] = jnp.zeros_like(small)
    for i in range(3):
        small[i * 3 : i * 3 + 3, :] = smoother_ref[0, 0, i].astype(f32)
    lanes = iota((16, 9 * vec), 1)
    starts = iota((16, 9 * vec), 0) * vec
    spread = dot_first(
        small[...].astype(bf16), ones_where((lanes >= starts) & (lanes < starts + vec))
    )
    for q in range(9):
        for n in range(nb):
            factors[q, n] = damping * spread[n * gr : (n + 1) * gr, q * vec : (q + 1) * vec]

    def smooth(n, value):
        v = [value[j * gr : (j + 1) * gr] for j in range(3)]
        return jnp.concatenate(
            [
                factors[3 * i, n] * v[0]
                + factors[3 * i + 1, n] * v[1]
                + factors[3 * i + 2, n] * v[2]
                for i in range(3)
            ],
            axis=0,
        )

    def loop(low, high, body, unroll=UNROLL):
        def several(step, carry):
            for u in range(unroll):
                body(low + step * unroll + u)
            return carry

        lax.fori_loop(0, (high - low) // unroll, several, 0)

    def multiply(n, source):
        picked = jnp.concatenate([source[col_ref[0, 0, k, n]] for k in range(kk)], axis=0)
        return dot(blocks[n], picked)

    def halo(packed, source, send_sem, recv_sem):
        return [
            pltpu.make_async_remote_copy(
                src_ref=packed.at[g],
                dst_ref=source.at[pl.ds(nb + g * hb, hb)],
                send_sem=send_sem.at[g],
                recv_sem=recv_sem.at[g],
                device_id=targets[g],
                device_id_type=MESH,
            )
            for g in range(4)
        ]

    def first_body(n):
        value = smooth(n, rhs[n])
        first[n] = value
        source1[n] = value.astype(bf16)

    halo1 = halo(packed1, source1, h1_send, h1_recv)
    for load in loads[1:]:
        load.wait()
    for g in range(4):
        for j in range(hb):
            n = send_ref[0, 0, g, j]
            packed1[g, j] = smooth(n, rhs[n]).astype(bf16)
        if g == 0:
            pl.semaphore_wait(barrier, len(greeted))
        halo1[g].start()
    loop(0, nb, first_body)

    wide[...] = jnp.zeros_like(wide)
    wide[0:cd, :] = prolong_ref[0, 0].astype(f32)
    rows, modes = iota((32, 8), 0), iota((32, 8), 1)
    hit = rows < 0
    for a in range(agg):
        hit = hit | ((rows == modes + a * cd) & (modes < cd))
    lane = iota((1, nb * dof), 1)
    owner = jnp.zeros((1, nb * dof), jnp.int32)
    for n in range(nb):
        owner = jnp.where(
            (lane >= n * dof) & (lane < (n + 1) * dof), agg_ref[0, 0, n] * cd, owner
        )
    owner = jnp.broadcast_to(owner, (32, nb * dof))
    unknown = iota((32, nb * dof), 0)
    expanded = dot(ones_where(hit), wide[...].astype(bf16))
    pexpt[...] = jnp.where(
        (unknown >= owner) & (unknown < owner + cd), expanded, 0.0
    ).astype(bf16)
    upright = dot_first(pexpt[...], ones_where(iota((32, vec), 0) == iota((32, vec), 1)))
    for n in range(nb):
        source3[n] = upright[n * dof : (n + 1) * dof].astype(bf16)
    modes, origin = iota((32, vec), 0), iota((32, vec), 1)
    for g in range(4):
        total = jnp.zeros((32, dof), f32)
        for j in range(hb):
            n = send_ref[0, 0, g, j]
            hit = modes < 0
            for a in range(agg):
                hit = hit | (origin - a * cd == modes - j * cd)
            hit = hit & (modes >= j * cd) & (modes < (j + 1) * cd) & (origin < cu)
            total = total + lax.dot_general(
                ones_where(hit), source3[n], (((1,), (1,)), ((), ())), preferred_element_type=f32
            )
            shift = (agg_ref[0, 0, n] * cd).astype(f32)
            total = jnp.where(iota((32, dof), 0) == cu + j, shift, total)
        pmsg[g] = total.astype(bf16)

    cinv32[...] = cinv_ref[...].astype(f32)

    def coarse_rows(c):
        return cinv32[pl.ds(pl.multiple_of(c * cu, 8), cu), :]

    cstack[...] = jnp.zeros_like(cstack)
    cstack[0:cu] = coarse_rows(col)
    cstack[3 * cu : 4 * cu] = coarse_rows(col_down)
    cstack[4 * cu : 5 * cu] = coarse_rows(col_up)
    crow[...] = cstack[0:32].astype(bf16)

    for copy in halo1:
        copy.wait_recv()
    pmsg_copies = [
        pltpu.make_async_remote_copy(
            src_ref=pmsg.at[g],
            dst_ref=pghost.at[g],
            send_sem=p_send.at[g],
            recv_sem=p_recv.at[g],
            device_id=targets[g],
            device_id_type=MESH,
        )
        for g in range(4)
    ]
    for copy in pmsg_copies:
        copy.start()

    for load in load_blocks:
        load.wait()

    def second_body(n):
        value = rhs[n] - multiply(n, source1)
        res[n] = value
        update = smooth(n, value)
        later[n] = first[n] + update
        source2[n] = update.astype(bf16)
        local[n] = update.astype(bf16)

    halo2 = [
        pltpu.make_async_remote_copy(
            src_ref=packed2.at[g, j],
            dst_ref=source2.at[nb + g * hb + j],
            send_sem=h2_send.at[g * hb + j],
            recv_sem=h2_recv.at[g * hb + j],
            device_id=targets[g],
            device_id_type=MESH,
        )
        for g in range(4)
        for j in range(hb)
    ]
    for j in range(hb):
        for g in range(2):
            n = send_ref[0, 0, g, j]
            packed2[g, j] = smooth(n, rhs[n] - multiply(n, source1)).astype(bf16)
            halo2[g * hb + j].start()
    loop(0, nb, second_body)
    for g in range(2, 4):
        for j in range(hb):
            packed2[g, j] = local[send_ref[0, 0, g, j]]
            halo2[g * hb + j].start()


    for copy in pmsg_copies:
        copy.wait_recv()
    for g in range(4):
        message = pghost[g]
        wide_message = message.astype(f32)
        for j in range(hb):
            shift = wide_message[cu + j : cu + j + 1, 0:vec]
            column = (origin - (1 + g) * cu - (modes - j * cd)).astype(f32)
            hit = (column == shift) & (modes >= j * cd) & (modes < (j + 1) * cd)
            source3[nb + g * hb + j] = dot_first(message, ones_where(hit)).astype(bf16)

    def operator_body(n):
        value = source3[n].astype(f32) - smooth(n, multiply(n, source3))
        high = value.astype(bf16)
        quick[n, :, 0:vec] = high
        quick[n, :, vec : 2 * vec] = (value - high.astype(f32)).astype(bf16)

    half = nb // 2
    loop(0, half, operator_body, 3)
    for copy in halo2:
        copy.wait_recv()
    crow_copies = [
        pltpu.make_async_remote_copy(
            src_ref=crow,
            dst_ref=cghost.at[g],
            send_sem=c_send.at[g],
            recv_sem=c_recv.at[g],
            device_id=targets[g],
            device_id_type=MESH,
        )
        for g in range(2)
    ]
    for copy in crow_copies:
        copy.start()
    def third_body(n):
        value = res[n] - multiply(n, source2)
        res[n] = value
        residual_low[pl.ds(pl.multiple_of(n * dof, dof), dof), :] = value.astype(bf16)

    loop(0, nb, third_body)
    gathered[at1, at2, col] = dot(pexpt[...], residual_low[...]).astype(bf16)

    def step_copies(line, pick, mine, others, send_sem, recv_sem):
        sends, arrivals = [], []
        for d, target in enumerate(line):
            sends.append(
                pltpu.make_async_remote_copy(
                    src_ref=pick(mine),
                    dst_ref=pick(mine),
                    send_sem=send_sem.at[d],
                    recv_sem=recv_sem.at[d],
                    device_id=target,
                    device_id_type=MESH,
                )
            )
            arrivals.append(
                pltpu.make_async_remote_copy(
                    src_ref=pick(mine),
                    dst_ref=pick(others[d]),
                    send_sem=send_sem.at[d],
                    recv_sem=recv_sem.at[d],
                    device_id=target,
                    device_id_type=MESH,
                )
            )
        return sends, arrivals

    def behind(at, count):
        return [(at + count - d) % count for d in range(1, count)]

    a_sends, a_arrivals = step_copies(
        line_a, lambda i: gathered.at[i, at2, col], at1, behind(at1, f1), ga_send, ga_recv
    )
    b_sends, b_arrivals = step_copies(
        line_b, lambda i: gathered.at[:, i, col], at2, behind(at2, f2), gb_send, gb_recv
    )
    c_sends, c_arrivals = step_copies(
        line_c, lambda i: gathered.at[:, :, i], col, behind(col, n_col), gc_send, gc_recv
    )
    for copy in a_sends:
        copy.start()

    def fourth_body(n):
        later[n] = later[n] + smooth(n, res[n])

    for copy in a_arrivals:
        copy.wait_recv()
    for copy in b_sends:
        copy.start()
    loop(0, nb, fourth_body, 4)
    write_later = pltpu.make_async_copy(later, later_ref, out_sem.at[0])
    write_later.start()
    loop(half, nb, operator_body, 3)
    write_quick = pltpu.make_async_copy(quick, quick_ref, out_sem.at[1])
    write_quick.start()
    for copy in b_arrivals:
        copy.wait_recv()
    for copy in c_sends:
        copy.start()
    for copy in crow_copies:
        copy.wait_recv()
    cstack[cu : 2 * cu] = cghost[0].astype(f32)[0:cu]
    cstack[2 * cu : 3 * cu] = cghost[1].astype(f32)[0:cu]
    for copy in c_arrivals:
        copy.wait_recv()

    def unpad(step, carry):
        for c in range(n_col):
            start = pl.multiple_of((step * n_col + c) * cu, 8)
            grhs[pl.ds(start, cu), :] = gathered[step // f2, step % f2, c].astype(f32)[0:cu]
        return carry

    lax.fori_loop(0, n_row, unpad, 0)
    coarse = dot(cstack[...].astype(bf16), grhs[...].astype(bf16)).astype(bf16)
    twice_ref[0:vec, :] = coarse
    twice_ref[vec : 2 * vec, :] = coarse
    for copy in halo1 + crow_copies + halo2 + pmsg_copies + a_sends + b_sends + c_sends:
        copy.wait_send()
    write_later.wait()
    write_quick.wait()


def body(rhs, smoother, blocks, col_index, send_list, agg_id, prolong, coarse_inverse):
    n_row, n_col = lax.axis_size("row"), lax.axis_size("col")
    nb, dof, vec = rhs.shape[2:]
    kk = col_index.shape[3]
    hb = send_list.shape[3]
    cd = prolong.shape[2]
    nc = coarse_inverse.shape[1]
    agg = nc // (n_row * n_col) // cd
    cu = agg * cd
    f2 = 4 if n_row % 4 == 0 else 1
    f1 = n_row // f2
    dims = (n_row, n_col, f1, f2, nb, dof, vec, kk, cd, agg, hb)
    slots = nb + 4 * hb
    field = (nb, dof, vec)
    dma = pltpu.SemaphoreType.DMA
    vmem = pl.BlockSpec(memory_space=pltpu.VMEM)
    anywhere = pl.BlockSpec(memory_space=pl.ANY)
    pinned = pl.BlockSpec(memory_space=pltpu.HBM)
    columns = jnp.swapaxes(col_index, 2, 3)
    later, quick, twice = pl.pallas_call(
        functools.partial(kernel, dims),
        out_shape=[
            jax.ShapeDtypeStruct(field, f32),
            jax.ShapeDtypeStruct((nb, dof, 2 * vec), bf16),
            jax.ShapeDtypeStruct((2 * vec, vec), bf16),
        ],
        in_specs=[pinned] * 8,
        out_specs=[anywhere, anywhere, vmem],
        scratch_shapes=[
            pltpu.VMEM(rhs.shape, f32),
            pltpu.VMEM(smoother.shape, bf16),
            pltpu.SMEM(columns.shape, jnp.int32),
            pltpu.SMEM(send_list.shape, jnp.int32),
            pltpu.SMEM(agg_id.shape, jnp.int32),
            pltpu.VMEM(prolong.shape, bf16),
            pltpu.VMEM(coarse_inverse.shape, bf16),
            pltpu.VMEM(blocks.shape[2:], bf16),
            pltpu.VMEM(field, f32),
            pltpu.VMEM(field, f32),
            pltpu.VMEM(field, f32),
            pltpu.VMEM((9, nb, dof // 3, vec), f32),
            pltpu.VMEM((16, nb * dof // 3), f32),
            pltpu.VMEM((8, nb * dof), f32),
            pltpu.VMEM((slots, dof, vec), bf16),
            pltpu.VMEM((slots, dof, vec), bf16),
            pltpu.VMEM((slots, dof, vec), bf16),
            pltpu.VMEM((4, hb, dof, vec), bf16),
            pltpu.VMEM((4, hb, dof, vec), bf16),
            pltpu.VMEM((4, 32, dof), bf16),
            pltpu.VMEM((4, 32, dof), bf16),
            pltpu.VMEM((n_col * cu, nc), f32),
            pltpu.VMEM((32, nc), bf16),
            pltpu.VMEM((2, 32, nc), bf16),
            pltpu.VMEM((vec, nc), f32),
            pltpu.VMEM((nb * dof, vec), bf16),
            pltpu.VMEM((32, nb * dof), bf16),
            pltpu.VMEM((f1, f2, n_col, 32, vec), bf16),
            pltpu.VMEM((nc, vec), f32),
            pltpu.VMEM((nb, dof, 2 * vec), bf16),
            pltpu.VMEM(field, bf16),
            dma((11,)),
            dma((2,)),
            dma((4,)),
            dma((4,)),
            dma((4 * hb,)),
            dma((4 * hb,)),
            dma((4,)),
            dma((4,)),
            dma((2,)),
            dma((2,)),
            dma((max(f1 - 1, 1),)),
            dma((max(f1 - 1, 1),)),
            dma((max(f2 - 1, 1),)),
            dma((max(f2 - 1, 1),)),
            dma((n_col - 1,)),
            dma((n_col - 1,)),
        ],
        compiler_params=pltpu.CompilerParams(
            collective_id=0, has_side_effects=True, vmem_limit_bytes=57 * 1024 * 1024
        ),
    )(rhs, smoother, blocks, columns, send_list, agg_id, prolong, coarse_inverse)
    return (later + dot(quick, twice))[None, None]


def solution(mesh):
    placed = (
        P("row", "col", None, None, None),
        P("row", "col", None, None, None),
        P("row", "col", None, None, None),
        P("row", "col", None, None),
        P("row", "col", None, None),
        P("row", "col", None),
        P("row", "col", None, None),
        P("row", None),
    )
    return jax.shard_map(
        body,
        mesh=mesh,
        in_specs=placed,
        out_specs=P("row", "col", None, None, None),
        check_vma=False,
    )
```

```python
import functools

import jax
import jax.numpy as jnp
from jax import lax
from jax.experimental import pallas as pl
from jax.experimental.pallas import tpu as pltpu
from jax.sharding import PartitionSpec as P

damping = 0.6
f32 = jnp.float32
bf16 = jnp.bfloat16
MESH = pl.DeviceIdType.MESH
UNROLL = 6


def iota(shape, axis):
    return lax.broadcasted_iota(jnp.int32, shape, axis)


def dot(a, b):
    return jnp.dot(a, b, preferred_element_type=f32)


def dot_first(a, b):
    return lax.dot_general(a, b, (((0,), (0,)), ((), ())), preferred_element_type=f32)


def ones_where(condition):
    return jnp.where(condition, 1.0, 0.0).astype(bf16)


def kernel(
    dims,
    rhs_hbm, smoother_hbm, blocks_hbm, col_hbm, send_hbm, agg_hbm, prolong_hbm, cinv_hbm,
    later_ref, quick_ref, twice_ref,
    rhs_ref, smoother_ref, col_ref, send_ref, agg_ref, prolong_ref, cinv_ref,
    blocks, first, res, later, factors, small, wide,
    source1, source2, source3, packed1, packed2, pmsg, pghost, cinv32, crow, cghost, cstack,
    residual_low, pexpt, reduced, gathered, grhs, quick, local,
    load_sem, out_sem, h1_send, h1_recv, h2_send, h2_recv, p_send, p_recv, c_send, c_recv,
    ga_send, ga_recv, gb_send, gb_recv, gc_send, gc_recv,
):
    n_row, n_col, f1, f2, nb, dof, vec, kk, cd, agg, hb = dims
    gr = dof // 3
    cu = cd * agg
    row, col = lax.axis_index("row"), lax.axis_index("col")
    at1, at2 = row // f2, row % f2

    loads = [
        pltpu.make_async_copy(source, target, load_sem.at[4 + at])
        for at, (source, target) in enumerate(
            [
                (smoother_hbm, smoother_ref),
                (rhs_hbm, rhs_ref),
                (send_hbm, send_ref),
                (col_hbm, col_ref),
                (agg_hbm, agg_ref),
                (prolong_hbm, prolong_ref),
                (cinv_hbm, cinv_ref),
            ]
        )
    ]
    for load in loads:
        load.start()
    rhs = rhs_ref.at[0, 0]
    parts = 4
    load_blocks = [
        pltpu.make_async_copy(
            blocks_hbm.at[0, 0, pl.ds(p * (nb // parts), nb // parts)],
            blocks.at[pl.ds(p * (nb // parts), nb // parts)],
            load_sem.at[p],
        )
        for p in range(parts)
    ]
    for load in load_blocks:
        load.start()

    row_up, row_down = (row + 1) % n_row, (row + n_row - 1) % n_row
    col_up, col_down = (col + 1) % n_col, (col + n_col - 1) % n_col
    targets = [(row_up, col), (row_down, col), (row, col_up), (row, col_down)]
    line_a = [((at1 + d) % f1 * f2 + at2, col) for d in range(1, f1)]
    line_b = [(at1 * f2 + (at2 + d) % f2, col) for d in range(1, f2)]
    line_c = [(row, (col + d) % n_col) for d in range(1, n_col)]
    greeted = targets + line_a + line_b + line_c
    barrier = pltpu.get_barrier_semaphore()
    for other in greeted:
        pl.semaphore_signal(barrier, inc=1, device_id=other, device_id_type=MESH)

    loads[0].wait()
    small[...] = jnp.zeros_like(small)
    for i in range(3):
        small[i * 3 : i * 3 + 3, :] = smoother_ref[0, 0, i].astype(f32)
    lanes = iota((16, 9 * vec), 1)
    starts = iota((16, 9 * vec), 0) * vec
    spread = dot_first(
        small[...].astype(bf16), ones_where((lanes >= starts) & (lanes < starts + vec))
    )
    for q in range(9):
        for n in range(nb):
            factors[q, n] = damping * spread[n * gr : (n + 1) * gr, q * vec : (q + 1) * vec]

    def smooth(n, value):
        v = [value[j * gr : (j + 1) * gr] for j in range(3)]
        return jnp.concatenate(
            [
                factors[3 * i, n] * v[0]
                + factors[3 * i + 1, n] * v[1]
                + factors[3 * i + 2, n] * v[2]
                for i in range(3)
            ],
            axis=0,
        )

    def loop(low, high, body, unroll=UNROLL):
        def several(step, carry):
            for u in range(unroll):
                body(low + step * unroll + u)
            return carry

        lax.fori_loop(0, (high - low) // unroll, several, 0)

    def multiply(n, source):
        picked = jnp.concatenate([source[col_ref[0, 0, k, n]] for k in range(kk)], axis=0)
        return dot(blocks[n], picked)

    def halo(packed, source, send_sem, recv_sem):
        return [
            pltpu.make_async_remote_copy(
                src_ref=packed.at[g],
                dst_ref=source.at[pl.ds(nb + g * hb, hb)],
                send_sem=send_sem.at[g],
                recv_sem=recv_sem.at[g],
                device_id=targets[g],
                device_id_type=MESH,
            )
            for g in range(4)
        ]

    def first_body(n):
        value = smooth(n, rhs[n])
        first[n] = value
        source1[n] = value.astype(bf16)

    halo1 = halo(packed1, source1, h1_send, h1_recv)
    for load in loads[1:]:
        load.wait()
    for g in range(4):
        for j in range(hb):
            n = send_ref[0, 0, g, j]
            packed1[g, j] = smooth(n, rhs[n]).astype(bf16)
        if g == 0:
            pl.semaphore_wait(barrier, len(greeted))
        halo1[g].start()
    loop(0, nb, first_body)

    wide[...] = jnp.zeros_like(wide)
    wide[0:cd, :] = prolong_ref[0, 0].astype(f32)
    rows, modes = iota((32, 8), 0), iota((32, 8), 1)
    hit = rows < 0
    for a in range(agg):
        hit = hit | ((rows == modes + a * cd) & (modes < cd))
    lane = iota((1, nb * dof), 1)
    owner = jnp.zeros((1, nb * dof), jnp.int32)
    for n in range(nb):
        owner = jnp.where(
            (lane >= n * dof) & (lane < (n + 1) * dof), agg_ref[0, 0, n] * cd, owner
        )
    owner = jnp.broadcast_to(owner, (32, nb * dof))
    unknown = iota((32, nb * dof), 0)
    expanded = dot(ones_where(hit), wide[...].astype(bf16))
    pexpt[...] = jnp.where(
        (unknown >= owner) & (unknown < owner + cd), expanded, 0.0
    ).astype(bf16)
    upright = dot_first(pexpt[...], ones_where(iota((32, vec), 0) == iota((32, vec), 1)))
    for n in range(nb):
        source3[n] = upright[n * dof : (n + 1) * dof].astype(bf16)
    modes, origin = iota((32, vec), 0), iota((32, vec), 1)
    for g in range(4):
        total = jnp.zeros((32, dof), f32)
        for j in range(hb):
            n = send_ref[0, 0, g, j]
            hit = modes < 0
            for a in range(agg):
                hit = hit | (origin - a * cd == modes - j * cd)
            hit = hit & (modes >= j * cd) & (modes < (j + 1) * cd) & (origin < cu)
            total = total + lax.dot_general(
                ones_where(hit), source3[n], (((1,), (1,)), ((), ())), preferred_element_type=f32
            )
            shift = (agg_ref[0, 0, n] * cd).astype(f32)
            total = jnp.where(iota((32, dof), 0) == cu + j, shift, total)
        pmsg[g] = total.astype(bf16)

    pmsg_copies = [
        pltpu.make_async_remote_copy(
            src_ref=pmsg.at[g],
            dst_ref=pghost.at[g],
            send_sem=p_send.at[g],
            recv_sem=p_recv.at[g],
            device_id=targets[g],
            device_id_type=MESH,
        )
        for g in range(4)
    ]
    for copy in pmsg_copies:
        copy.start()

    for load in load_blocks:
        load.wait()

    def reduced_body(n):
        value = dot_first(source3[n][:, 0:32], blocks[n])
        high = value.astype(bf16)
        reduced[n, 0:32, :] = high
        reduced[n, 32:64, :] = (value - high.astype(f32)).astype(bf16)

    loop(0, nb, reduced_body)
    cinv32[...] = cinv_ref[...].astype(f32)

    def coarse_rows(c):
        return cinv32[pl.ds(pl.multiple_of(c * cu, 8), cu), :]

    cstack[...] = jnp.zeros_like(cstack)
    cstack[0:cu] = coarse_rows(col)
    cstack[3 * cu : 4 * cu] = coarse_rows(col_down)
    cstack[4 * cu : 5 * cu] = coarse_rows(col_up)
    crow[...] = cstack[0:32].astype(bf16)

    def operator_body(n):
        value = source3[n].astype(f32) - smooth(n, multiply(n, source3))
        high = value.astype(bf16)
        quick[n, :, 0:vec] = high
        quick[n, :, vec : 2 * vec] = (value - high.astype(f32)).astype(bf16)

    half = nb // 2
    for copy in halo1:
        copy.wait_recv()

    def second_body(n):
        value = rhs[n] - multiply(n, source1)
        res[n] = value
        update = smooth(n, value)
        later[n] = first[n] + update
        high = value.astype(bf16)
        place = pl.ds(pl.multiple_of(n * dof, dof), dof)
        residual_low[0, place, :] = high
        residual_low[1, place, :] = (value - high.astype(f32)).astype(bf16)
        source2[n] = update.astype(bf16)
        local[n] = update.astype(bf16)

    halo2 = [
        pltpu.make_async_remote_copy(
            src_ref=packed2.at[g, j],
            dst_ref=source2.at[nb + g * hb + j],
            send_sem=h2_send.at[g * hb + j],
            recv_sem=h2_recv.at[g * hb + j],
            device_id=targets[g],
            device_id_type=MESH,
        )
        for g in range(4)
        for j in range(hb)
    ]
    for j in range(hb):
        for g in range(2):
            n = send_ref[0, 0, g, j]
            packed2[g, j] = smooth(n, rhs[n] - multiply(n, source1)).astype(bf16)
            halo2[g * hb + j].start()
    loop(0, nb, second_body)
    for g in range(2, 4):
        for j in range(hb):
            packed2[g, j] = local[send_ref[0, 0, g, j]]
            halo2[g * hb + j].start()

    before = dot(pexpt[...], residual_low[0]) + dot(pexpt[...], residual_low[1])
    for copy in pmsg_copies:
        copy.wait_recv()
    for g in range(4):
        message = pghost[g]
        wide_message = message.astype(f32)
        for j in range(hb):
            shift = wide_message[cu + j : cu + j + 1, 0:vec]
            column = (origin - (1 + g) * cu - (modes - j * cd)).astype(f32)
            hit = (column == shift) & (modes >= j * cd) & (modes < (j + 1) * cd)
            source3[nb + g * hb + j] = dot_first(message, ones_where(hit)).astype(bf16)

    loop(0, half, operator_body, 3)
    for copy in halo2:
        copy.wait_recv()
    crow_copies = [
        pltpu.make_async_remote_copy(
            src_ref=crow,
            dst_ref=cghost.at[g],
            send_sem=c_send.at[g],
            recv_sem=c_recv.at[g],
            device_id=targets[g],
            device_id_type=MESH,
        )
        for g in range(2)
    ]
    for copy in crow_copies:
        copy.start()

    def take_off(step, total):
        for u in range(UNROLL):
            n = step * UNROLL + u
            picked = jnp.concatenate([source2[col_ref[0, 0, k, n]] for k in range(kk)], axis=0)
            total = total - dot(reduced[n], picked)
        return total

    taken = lax.fori_loop(0, nb // UNROLL, take_off, jnp.zeros((64, vec), f32))
    gathered[at1, at2, col] = (before + (taken[0:32] + taken[32:64])).astype(bf16)

    def step_copies(line, pick, mine, others, send_sem, recv_sem):
        sends, arrivals = [], []
        for d, target in enumerate(line):
            sends.append(
                pltpu.make_async_remote_copy(
                    src_ref=pick(mine),
                    dst_ref=pick(mine),
                    send_sem=send_sem.at[d],
                    recv_sem=recv_sem.at[d],
                    device_id=target,
                    device_id_type=MESH,
                )
            )
            arrivals.append(
                pltpu.make_async_remote_copy(
                    src_ref=pick(mine),
                    dst_ref=pick(others[d]),
                    send_sem=send_sem.at[d],
                    recv_sem=recv_sem.at[d],
                    device_id=target,
                    device_id_type=MESH,
                )
            )
        return sends, arrivals

    def behind(at, count):
        return [(at + count - d) % count for d in range(1, count)]

    a_sends, a_arrivals = step_copies(
        line_a, lambda i: gathered.at[i, at2, col], at1, behind(at1, f1), ga_send, ga_recv
    )
    b_sends, b_arrivals = step_copies(
        line_b, lambda i: gathered.at[:, i, col], at2, behind(at2, f2), gb_send, gb_recv
    )
    c_sends, c_arrivals = step_copies(
        line_c, lambda i: gathered.at[:, :, i], col, behind(col, n_col), gc_send, gc_recv
    )
    for copy in a_sends:
        copy.start()

    def fourth_body(n):
        later[n] = later[n] + smooth(n, res[n] - multiply(n, source2))

    loop(half, nb, operator_body, 3)
    write_quick = pltpu.make_async_copy(quick, quick_ref, out_sem.at[1])
    write_quick.start()
    for copy in a_arrivals:
        copy.wait_recv()
    for copy in b_sends:
        copy.start()
    loop(0, half, fourth_body, 3)
    for copy in b_arrivals:
        copy.wait_recv()
    for copy in c_sends:
        copy.start()
    for copy in crow_copies:
        copy.wait_recv()
    cstack[cu : 2 * cu] = cghost[0].astype(f32)[0:cu]
    cstack[2 * cu : 3 * cu] = cghost[1].astype(f32)[0:cu]
    loop(half, nb, fourth_body, 3)
    write_later = pltpu.make_async_copy(later, later_ref, out_sem.at[0])
    write_later.start()
    for copy in c_arrivals:
        copy.wait_recv()

    def unpad(step, carry):
        for c in range(n_col):
            start = pl.multiple_of((step * n_col + c) * cu, 8)
            grhs[pl.ds(start, cu), :] = gathered[step // f2, step % f2, c].astype(f32)[0:cu]
        return carry

    lax.fori_loop(0, n_row, unpad, 0)
    coarse = dot(cstack[...].astype(bf16), grhs[...].astype(bf16)).astype(bf16)
    twice_ref[0:vec, :] = coarse
    twice_ref[vec : 2 * vec, :] = coarse
    for copy in halo1 + crow_copies + halo2 + pmsg_copies + a_sends + b_sends + c_sends:
        copy.wait_send()
    write_later.wait()
    write_quick.wait()


def finish(later_ref, quick_ref, twice_ref, out_ref):
    for n in range(later_ref.shape[0]):
        out_ref[0, 0, n] = later_ref[n] + dot(quick_ref[n], twice_ref[...])


def body(rhs, smoother, blocks, col_index, send_list, agg_id, prolong, coarse_inverse):
    n_row, n_col = lax.axis_size("row"), lax.axis_size("col")
    nb, dof, vec = rhs.shape[2:]
    kk = col_index.shape[3]
    hb = send_list.shape[3]
    cd = prolong.shape[2]
    nc = coarse_inverse.shape[1]
    agg = nc // (n_row * n_col) // cd
    cu = agg * cd
    f2 = 4 if n_row % 4 == 0 else 1
    f1 = n_row // f2
    dims = (n_row, n_col, f1, f2, nb, dof, vec, kk, cd, agg, hb)
    slots = nb + 4 * hb
    field = (nb, dof, vec)
    dma = pltpu.SemaphoreType.DMA
    vmem = pl.BlockSpec(memory_space=pltpu.VMEM)
    anywhere = pl.BlockSpec(memory_space=pl.ANY)
    pinned = pl.BlockSpec(memory_space=pltpu.HBM)
    columns = jnp.swapaxes(col_index, 2, 3)
    later, quick, twice = pl.pallas_call(
        functools.partial(kernel, dims),
        out_shape=[
            jax.ShapeDtypeStruct(field, f32),
            jax.ShapeDtypeStruct((nb, dof, 2 * vec), bf16),
            jax.ShapeDtypeStruct((2 * vec, vec), bf16),
        ],
        in_specs=[pinned] * 8,
        out_specs=[anywhere, anywhere, vmem],
        scratch_shapes=[
            pltpu.VMEM(rhs.shape, f32),
            pltpu.VMEM(smoother.shape, bf16),
            pltpu.SMEM(columns.shape, jnp.int32),
            pltpu.SMEM(send_list.shape, jnp.int32),
            pltpu.SMEM(agg_id.shape, jnp.int32),
            pltpu.VMEM(prolong.shape, bf16),
            pltpu.VMEM(coarse_inverse.shape, bf16),
            pltpu.VMEM(blocks.shape[2:], bf16),
            pltpu.VMEM(field, f32),
            pltpu.VMEM(field, f32),
            pltpu.VMEM(field, f32),
            pltpu.VMEM((9, nb, dof // 3, vec), f32),
            pltpu.VMEM((16, nb * dof // 3), f32),
            pltpu.VMEM((8, nb * dof), f32),
            pltpu.VMEM((slots, dof, vec), bf16),
            pltpu.VMEM((slots, dof, vec), bf16),
            pltpu.VMEM((slots, dof, vec), bf16),
            pltpu.VMEM((4, hb, dof, vec), bf16),
            pltpu.VMEM((4, hb, dof, vec), bf16),
            pltpu.VMEM((4, 32, dof), bf16),
            pltpu.VMEM((4, 32, dof), bf16),
            pltpu.VMEM((n_col * cu, nc), f32),
            pltpu.VMEM((32, nc), bf16),
            pltpu.VMEM((2, 32, nc), bf16),
            pltpu.VMEM((vec, nc), f32),
            pltpu.VMEM((2, nb * dof, vec), bf16),
            pltpu.VMEM((32, nb * dof), bf16),
            pltpu.VMEM((nb, 64, kk * dof), bf16),
            pltpu.VMEM((f1, f2, n_col, 32, vec), bf16),
            pltpu.VMEM((nc, vec), f32),
            pltpu.VMEM((nb, dof, 2 * vec), bf16),
            pltpu.VMEM(field, bf16),
            dma((11,)),
            dma((2,)),
            dma((4,)),
            dma((4,)),
            dma((4 * hb,)),
            dma((4 * hb,)),
            dma((4,)),
            dma((4,)),
            dma((2,)),
            dma((2,)),
            dma((max(f1 - 1, 1),)),
            dma((max(f1 - 1, 1),)),
            dma((max(f2 - 1, 1),)),
            dma((max(f2 - 1, 1),)),
            dma((n_col - 1,)),
            dma((n_col - 1,)),
        ],
        compiler_params=pltpu.CompilerParams(
            collective_id=0, has_side_effects=True, vmem_limit_bytes=57 * 1024 * 1024
        ),
    )(rhs, smoother, blocks, columns, send_list, agg_id, prolong, coarse_inverse)
    rows = 3 if nb % 3 == 0 else 1
    return pl.pallas_call(
        finish,
        grid=(nb // rows,),
        out_shape=jax.ShapeDtypeStruct(rhs.shape, f32),
        in_specs=[
            pl.BlockSpec((rows, dof, vec), lambda n: (n, 0, 0)),
            pl.BlockSpec((rows, dof, 2 * vec), lambda n: (n, 0, 0)),
            pl.BlockSpec((2 * vec, vec), lambda n: (0, 0)),
        ],
        out_specs=pl.BlockSpec((1, 1, rows, dof, vec), lambda n: (0, 0, n, 0, 0)),
        compiler_params=pltpu.CompilerParams(vmem_limit_bytes=57 * 1024 * 1024),
    )(later, quick, twice)


def solution(mesh):
    placed = (
        P("row", "col", None, None, None),
        P("row", "col", None, None, None),
        P("row", "col", None, None, None),
        P("row", "col", None, None),
        P("row", "col", None, None),
        P("row", "col", None),
        P("row", "col", None, None),
        P("row", None),
    )
    return jax.shard_map(
        body,
        mesh=mesh,
        in_specs=placed,
        out_specs=P("row", "col", None, None, None),
        check_vma=False,
    )
```

```python
import functools

import jax
import jax.numpy as jnp
from jax import lax
from jax.experimental import pallas as pl
from jax.experimental.pallas import tpu as pltpu
from jax.sharding import PartitionSpec as P

damping = 0.6
f32 = jnp.float32
bf16 = jnp.bfloat16
MESH = pl.DeviceIdType.MESH
UNROLL = 6


def iota(shape, axis):
    return lax.broadcasted_iota(jnp.int32, shape, axis)


def dot(a, b):
    return jnp.dot(a, b, preferred_element_type=f32)


def dot_first(a, b):
    return lax.dot_general(a, b, (((0,), (0,)), ((), ())), preferred_element_type=f32)


def ones_where(condition):
    return jnp.where(condition, 1.0, 0.0).astype(bf16)


def kernel(
    dims,
    rhs_hbm, smoother_hbm, blocks_hbm, col_hbm, send_hbm, agg_hbm, prolong_hbm, cinv_hbm,
    later_ref, quick_ref, twice_ref,
    rhs_ref, smoother_ref, col_ref, send_ref, agg_ref, prolong_ref, cinv_ref,
    blocks, first, res, later, factors, small, wide,
    source1, source2, source3, packed1, packed2, pmsg, pghost, cinv32, crow, cghost, cstack,
    residual_low, pexpt, reduced, gathered, grhs, quick, local,
    load_sem, out_sem, h1_send, h1_recv, h2_send, h2_recv, p_send, p_recv, c_send, c_recv,
    ga_send, ga_recv, gb_send, gb_recv, gc_send, gc_recv,
):
    n_row, n_col, f1, f2, nb, dof, vec, kk, cd, agg, hb = dims
    gr = dof // 3
    cu = cd * agg
    row, col = lax.axis_index("row"), lax.axis_index("col")
    at1, at2 = row // f2, row % f2

    loads = [
        pltpu.make_async_copy(source, target, load_sem.at[4 + at])
        for at, (source, target) in enumerate(
            [
                (smoother_hbm, smoother_ref),
                (rhs_hbm, rhs_ref),
                (send_hbm, send_ref),
                (col_hbm, col_ref),
                (agg_hbm, agg_ref),
                (prolong_hbm, prolong_ref),
                (cinv_hbm, cinv_ref),
            ]
        )
    ]
    for load in loads:
        load.start()
    rhs = rhs_ref.at[0, 0]
    parts = 4
    load_blocks = [
        pltpu.make_async_copy(
            blocks_hbm.at[0, 0, pl.ds(p * (nb // parts), nb // parts)],
            blocks.at[pl.ds(p * (nb // parts), nb // parts)],
            load_sem.at[p],
        )
        for p in range(parts)
    ]

    row_up, row_down = (row + 1) % n_row, (row + n_row - 1) % n_row
    col_up, col_down = (col + 1) % n_col, (col + n_col - 1) % n_col
    targets = [(row_up, col), (row_down, col), (row, col_up), (row, col_down)]
    line_a = [((at1 + d) % f1 * f2 + at2, col) for d in range(1, f1)]
    line_b = [(at1 * f2 + (at2 + d) % f2, col) for d in range(1, f2)]
    line_c = [(row, (col + d) % n_col) for d in range(1, n_col)]
    greeted = targets + line_a + line_b + line_c
    barrier = pltpu.get_barrier_semaphore()
    for other in greeted:
        pl.semaphore_signal(barrier, inc=1, device_id=other, device_id_type=MESH)

    loads[0].wait()
    small[...] = jnp.zeros_like(small)
    for i in range(3):
        small[i * 3 : i * 3 + 3, :] = smoother_ref[0, 0, i].astype(f32)
    lanes = iota((16, 9 * vec), 1)
    starts = iota((16, 9 * vec), 0) * vec
    spread = dot_first(
        small[...].astype(bf16), ones_where((lanes >= starts) & (lanes < starts + vec))
    )
    for q in range(9):
        for n in range(nb):
            factors[q, n] = damping * spread[n * gr : (n + 1) * gr, q * vec : (q + 1) * vec]

    def smooth(n, value):
        v = [value[j * gr : (j + 1) * gr] for j in range(3)]
        return jnp.concatenate(
            [
                factors[3 * i, n] * v[0]
                + factors[3 * i + 1, n] * v[1]
                + factors[3 * i + 2, n] * v[2]
                for i in range(3)
            ],
            axis=0,
        )

    def loop(low, high, body, unroll=UNROLL):
        def several(step, carry):
            for u in range(unroll):
                body(low + step * unroll + u)
            return carry

        lax.fori_loop(0, (high - low) // unroll, several, 0)

    def multiply(n, source):
        picked = jnp.concatenate([source[col_ref[0, 0, k, n]] for k in range(kk)], axis=0)
        return dot(blocks[n], picked)

    def halo(packed, source, send_sem, recv_sem):
        return [
            pltpu.make_async_remote_copy(
                src_ref=packed.at[g],
                dst_ref=source.at[pl.ds(nb + g * hb, hb)],
                send_sem=send_sem.at[g],
                recv_sem=recv_sem.at[g],
                device_id=targets[g],
                device_id_type=MESH,
            )
            for g in range(4)
        ]

    def first_body(n):
        value = smooth(n, rhs[n])
        first[n] = value
        source1[n] = value.astype(bf16)

    halo1 = halo(packed1, source1, h1_send, h1_recv)
    for load in loads[1:3]:
        load.wait()
    for load in load_blocks:
        load.start()
    for g in range(4):
        for j in range(hb):
            n = send_ref[0, 0, g, j]
            packed1[g, j] = smooth(n, rhs[n]).astype(bf16)
        if g == 0:
            pl.semaphore_wait(barrier, len(greeted))
        halo1[g].start()
    loop(0, nb, first_body)

    for load in loads[3:]:
        load.wait()
    wide[...] = jnp.zeros_like(wide)
    wide[0:cd, :] = prolong_ref[0, 0].astype(f32)
    rows, modes = iota((32, 8), 0), iota((32, 8), 1)
    hit = rows < 0
    for a in range(agg):
        hit = hit | ((rows == modes + a * cd) & (modes < cd))
    lane = iota((1, nb * dof), 1)
    owner = jnp.zeros((1, nb * dof), jnp.int32)
    for n in range(nb):
        owner = jnp.where(
            (lane >= n * dof) & (lane < (n + 1) * dof), agg_ref[0, 0, n] * cd, owner
        )
    owner = jnp.broadcast_to(owner, (32, nb * dof))
    unknown = iota((32, nb * dof), 0)
    expanded = dot(ones_where(hit), wide[...].astype(bf16))
    pexpt[...] = jnp.where(
        (unknown >= owner) & (unknown < owner + cd), expanded, 0.0
    ).astype(bf16)
    upright = dot_first(pexpt[...], ones_where(iota((32, vec), 0) == iota((32, vec), 1)))
    for n in range(nb):
        source3[n] = upright[n * dof : (n + 1) * dof].astype(bf16)
    modes, origin = iota((32, vec), 0), iota((32, vec), 1)
    for g in range(4):
        total = jnp.zeros((32, dof), f32)
        for j in range(hb):
            n = send_ref[0, 0, g, j]
            hit = modes < 0
            for a in range(agg):
                hit = hit | (origin - a * cd == modes - j * cd)
            hit = hit & (modes >= j * cd) & (modes < (j + 1) * cd) & (origin < cu)
            total = total + lax.dot_general(
                ones_where(hit), source3[n], (((1,), (1,)), ((), ())), preferred_element_type=f32
            )
            shift = (agg_ref[0, 0, n] * cd).astype(f32)
            total = jnp.where(iota((32, dof), 0) == cu + j, shift, total)
        pmsg[g] = total.astype(bf16)

    pmsg_copies = [
        pltpu.make_async_remote_copy(
            src_ref=pmsg.at[g],
            dst_ref=pghost.at[g],
            send_sem=p_send.at[g],
            recv_sem=p_recv.at[g],
            device_id=targets[g],
            device_id_type=MESH,
        )
        for g in range(4)
    ]
    for copy in pmsg_copies:
        copy.start()

    for load in load_blocks:
        load.wait()

    def reduced_body(n):
        value = dot_first(source3[n][:, 0:32], blocks[n])
        high = value.astype(bf16)
        reduced[n, 0:32, :] = high
        reduced[n, 32:64, :] = (value - high.astype(f32)).astype(bf16)

    loop(0, nb, reduced_body)
    cinv32[...] = cinv_ref[...].astype(f32)

    def coarse_rows(c):
        return cinv32[pl.ds(pl.multiple_of(c * cu, 8), cu), :]

    cstack[...] = jnp.zeros_like(cstack)
    cstack[0:cu] = coarse_rows(col)
    cstack[3 * cu : 4 * cu] = coarse_rows(col_down)
    cstack[4 * cu : 5 * cu] = coarse_rows(col_up)
    crow[...] = cstack[0:32].astype(bf16)

    def operator_body(n):
        value = source3[n].astype(f32) - smooth(n, multiply(n, source3))
        high = value.astype(bf16)
        quick[n, :, 0:vec] = high
        quick[n, :, vec : 2 * vec] = (value - high.astype(f32)).astype(bf16)

    half = nb // 2
    for copy in halo1:
        copy.wait_recv()

    def second_body(n):
        value = rhs[n] - multiply(n, source1)
        res[n] = value
        update = smooth(n, value)
        later[n] = first[n] + update
        high = value.astype(bf16)
        place = pl.ds(pl.multiple_of(n * dof, dof), dof)
        residual_low[0, place, :] = high
        residual_low[1, place, :] = (value - high.astype(f32)).astype(bf16)
        source2[n] = update.astype(bf16)
        local[n] = update.astype(bf16)

    halo2 = [
        pltpu.make_async_remote_copy(
            src_ref=packed2.at[g, j],
            dst_ref=source2.at[nb + g * hb + j],
            send_sem=h2_send.at[g * hb + j],
            recv_sem=h2_recv.at[g * hb + j],
            device_id=targets[g],
            device_id_type=MESH,
        )
        for g in range(4)
        for j in range(hb)
    ]
    for j in range(hb):
        for g in range(2):
            n = send_ref[0, 0, g, j]
            packed2[g, j] = smooth(n, rhs[n] - multiply(n, source1)).astype(bf16)
            halo2[g * hb + j].start()
    loop(0, nb, second_body)
    for g in range(2, 4):
        for j in range(hb):
            packed2[g, j] = local[send_ref[0, 0, g, j]]
            halo2[g * hb + j].start()

    before = dot(pexpt[...], residual_low[0]) + dot(pexpt[...], residual_low[1])
    for copy in pmsg_copies:
        copy.wait_recv()
    for g in range(4):
        message = pghost[g]
        wide_message = message.astype(f32)
        for j in range(hb):
            shift = wide_message[cu + j : cu + j + 1, 0:vec]
            column = (origin - (1 + g) * cu - (modes - j * cd)).astype(f32)
            hit = (column == shift) & (modes >= j * cd) & (modes < (j + 1) * cd)
            source3[nb + g * hb + j] = dot_first(message, ones_where(hit)).astype(bf16)

    loop(0, half, operator_body, 3)
    for copy in halo2:
        copy.wait_recv()
    crow_copies = [
        pltpu.make_async_remote_copy(
            src_ref=crow,
            dst_ref=cghost.at[g],
            send_sem=c_send.at[g],
            recv_sem=c_recv.at[g],
            device_id=targets[g],
            device_id_type=MESH,
        )
        for g in range(2)
    ]
    for copy in crow_copies:
        copy.start()

    def take_off(step, total):
        for u in range(UNROLL):
            n = step * UNROLL + u
            picked = jnp.concatenate([source2[col_ref[0, 0, k, n]] for k in range(kk)], axis=0)
            total = total - dot(reduced[n], picked)
        return total

    taken = lax.fori_loop(0, nb // UNROLL, take_off, jnp.zeros((64, vec), f32))
    gathered[at1, at2, col] = (before + (taken[0:32] + taken[32:64])).astype(bf16)

    def step_copies(line, pick, mine, others, send_sem, recv_sem):
        sends, arrivals = [], []
        for d, target in enumerate(line):
            sends.append(
                pltpu.make_async_remote_copy(
                    src_ref=pick(mine),
                    dst_ref=pick(mine),
                    send_sem=send_sem.at[d],
                    recv_sem=recv_sem.at[d],
                    device_id=target,
                    device_id_type=MESH,
                )
            )
            arrivals.append(
                pltpu.make_async_remote_copy(
                    src_ref=pick(mine),
                    dst_ref=pick(others[d]),
                    send_sem=send_sem.at[d],
                    recv_sem=recv_sem.at[d],
                    device_id=target,
                    device_id_type=MESH,
                )
            )
        return sends, arrivals

    def behind(at, count):
        return [(at + count - d) % count for d in range(1, count)]

    a_sends, a_arrivals = step_copies(
        line_a, lambda i: gathered.at[i, at2, col], at1, behind(at1, f1), ga_send, ga_recv
    )
    b_sends, b_arrivals = step_copies(
        line_b, lambda i: gathered.at[:, i, col], at2, behind(at2, f2), gb_send, gb_recv
    )
    c_sends, c_arrivals = step_copies(
        line_c, lambda i: gathered.at[:, :, i], col, behind(col, n_col), gc_send, gc_recv
    )
    for copy in a_sends:
        copy.start()

    def fourth_body(n):
        later[n] = later[n] + smooth(n, res[n] - multiply(n, source2))

    loop(half, nb, operator_body, 3)
    write_quick = pltpu.make_async_copy(quick, quick_ref, out_sem.at[1])
    write_quick.start()
    for copy in a_arrivals:
        copy.wait_recv()
    for copy in b_sends:
        copy.start()
    loop(0, half, fourth_body, 3)
    for copy in b_arrivals:
        copy.wait_recv()
    for copy in c_sends:
        copy.start()
    for copy in crow_copies:
        copy.wait_recv()
    cstack[cu : 2 * cu] = cghost[0].astype(f32)[0:cu]
    cstack[2 * cu : 3 * cu] = cghost[1].astype(f32)[0:cu]
    loop(half, nb, fourth_body, 3)
    write_later = pltpu.make_async_copy(later, later_ref, out_sem.at[0])
    write_later.start()
    cstack_low = cstack[...].astype(bf16)
    for copy in c_arrivals:
        copy.wait_recv()

    def unpad(step, carry):
        for c in range(n_col):
            start = pl.multiple_of((step * n_col + c) * cu, 8)
            grhs[pl.ds(start, cu), :] = gathered[step // f2, step % f2, c].astype(f32)[0:cu]
        return carry

    lax.fori_loop(0, n_row, unpad, 0)
    coarse = dot(cstack_low, grhs[...].astype(bf16)).astype(bf16)
    twice_ref[0:vec, :] = coarse
    twice_ref[vec : 2 * vec, :] = coarse
    for copy in halo1 + crow_copies + halo2 + pmsg_copies + a_sends + b_sends + c_sends:
        copy.wait_send()
    write_later.wait()
    write_quick.wait()


def body(rhs, smoother, blocks, col_index, send_list, agg_id, prolong, coarse_inverse):
    n_row, n_col = lax.axis_size("row"), lax.axis_size("col")
    nb, dof, vec = rhs.shape[2:]
    kk = col_index.shape[3]
    hb = send_list.shape[3]
    cd = prolong.shape[2]
    nc = coarse_inverse.shape[1]
    agg = nc // (n_row * n_col) // cd
    cu = agg * cd
    f2 = 4 if n_row % 4 == 0 else 1
    f1 = n_row // f2
    dims = (n_row, n_col, f1, f2, nb, dof, vec, kk, cd, agg, hb)
    slots = nb + 4 * hb
    field = (nb, dof, vec)
    dma = pltpu.SemaphoreType.DMA
    vmem = pl.BlockSpec(memory_space=pltpu.VMEM)
    anywhere = pl.BlockSpec(memory_space=pl.ANY)
    pinned = pl.BlockSpec(memory_space=pltpu.HBM)
    columns = jnp.swapaxes(col_index, 2, 3)
    later, quick, twice = pl.pallas_call(
        functools.partial(kernel, dims),
        out_shape=[
            jax.ShapeDtypeStruct(field, f32),
            jax.ShapeDtypeStruct((nb, dof, 2 * vec), bf16),
            jax.ShapeDtypeStruct((2 * vec, vec), bf16),
        ],
        in_specs=[pinned] * 8,
        out_specs=[anywhere, anywhere, vmem],
        scratch_shapes=[
            pltpu.VMEM(rhs.shape, f32),
            pltpu.VMEM(smoother.shape, bf16),
            pltpu.SMEM(columns.shape, jnp.int32),
            pltpu.SMEM(send_list.shape, jnp.int32),
            pltpu.SMEM(agg_id.shape, jnp.int32),
            pltpu.VMEM(prolong.shape, bf16),
            pltpu.VMEM(coarse_inverse.shape, bf16),
            pltpu.VMEM(blocks.shape[2:], bf16),
            pltpu.VMEM(field, f32),
            pltpu.VMEM(field, f32),
            pltpu.VMEM(field, f32),
            pltpu.VMEM((9, nb, dof // 3, vec), f32),
            pltpu.VMEM((16, nb * dof // 3), f32),
            pltpu.VMEM((8, nb * dof), f32),
            pltpu.VMEM((slots, dof, vec), bf16),
            pltpu.VMEM((slots, dof, vec), bf16),
            pltpu.VMEM((slots, dof, vec), bf16),
            pltpu.VMEM((4, hb, dof, vec), bf16),
            pltpu.VMEM((4, hb, dof, vec), bf16),
            pltpu.VMEM((4, 32, dof), bf16),
            pltpu.VMEM((4, 32, dof), bf16),
            pltpu.VMEM((n_col * cu, nc), f32),
            pltpu.VMEM((32, nc), bf16),
            pltpu.VMEM((2, 32, nc), bf16),
            pltpu.VMEM((vec, nc), f32),
            pltpu.VMEM((2, nb * dof, vec), bf16),
            pltpu.VMEM((32, nb * dof), bf16),
            pltpu.VMEM((nb, 64, kk * dof), bf16),
            pltpu.VMEM((f1, f2, n_col, 32, vec), bf16),
            pltpu.VMEM((nc, vec), f32),
            pltpu.VMEM((nb, dof, 2 * vec), bf16),
            pltpu.VMEM(field, bf16),
            dma((11,)),
            dma((2,)),
            dma((4,)),
            dma((4,)),
            dma((4 * hb,)),
            dma((4 * hb,)),
            dma((4,)),
            dma((4,)),
            dma((2,)),
            dma((2,)),
            dma((max(f1 - 1, 1),)),
            dma((max(f1 - 1, 1),)),
            dma((max(f2 - 1, 1),)),
            dma((max(f2 - 1, 1),)),
            dma((n_col - 1,)),
            dma((n_col - 1,)),
        ],
        compiler_params=pltpu.CompilerParams(
            collective_id=0, has_side_effects=True, vmem_limit_bytes=57 * 1024 * 1024
        ),
    )(rhs, smoother, blocks, columns, send_list, agg_id, prolong, coarse_inverse)
    return (later + dot(quick, twice))[None, None]


def solution(mesh):
    placed = (
        P("row", "col", None, None, None),
        P("row", "col", None, None, None),
        P("row", "col", None, None, None),
        P("row", "col", None, None),
        P("row", "col", None, None),
        P("row", "col", None),
        P("row", "col", None, None),
        P("row", None),
    )
    return jax.shard_map(
        body,
        mesh=mesh,
        in_specs=placed,
        out_specs=P("row", "col", None, None, None),
        check_vma=False,
    )
```

```python
import functools

import jax
import jax.numpy as jnp
from jax import lax
from jax.experimental import pallas as pl
from jax.experimental.pallas import tpu as pltpu
from jax.sharding import PartitionSpec as P

damping = 0.6
f32 = jnp.float32
bf16 = jnp.bfloat16
MESH = pl.DeviceIdType.MESH
UNROLL = 6


def iota(shape, axis):
    return lax.broadcasted_iota(jnp.int32, shape, axis)


def dot(a, b):
    return jnp.dot(a, b, preferred_element_type=f32)


def dot_first(a, b):
    return lax.dot_general(a, b, (((0,), (0,)), ((), ())), preferred_element_type=f32)


def ones_where(condition):
    return jnp.where(condition, 1.0, 0.0).astype(bf16)


def kernel(
    dims,
    rhs_hbm, smoother_hbm, blocks_hbm, col_hbm, send_hbm, agg_hbm, prolong_hbm, cinv_hbm,
    later_ref, quick_ref, twice_ref,
    rhs_ref, smoother_ref, col_ref, send_ref, agg_ref, prolong_ref, cinv_ref,
    blocks, first, res, later, factors, small, wide,
    source1, source2, source3, packed1, packed2, pmsg, pghost, cinv32, crow, cghost, cstack,
    residual_low, pexpt, reduced, gathered, grhs, quick, local,
    load_sem, out_sem, h1_send, h1_recv, h2_send, h2_recv, p_send, p_recv, c_send, c_recv,
    ga_send, ga_recv, gb_send, gb_recv, gc_send, gc_recv,
):
    n_row, n_col, f1, f2, nb, dof, vec, kk, cd, agg, hb = dims
    gr = dof // 3
    cu = cd * agg
    row, col = lax.axis_index("row"), lax.axis_index("col")
    at1, at2 = row // f2, row % f2

    loads = [
        pltpu.make_async_copy(source, target, load_sem.at[4 + at])
        for at, (source, target) in enumerate(
            [
                (smoother_hbm, smoother_ref),
                (rhs_hbm, rhs_ref),
                (send_hbm, send_ref),
                (col_hbm, col_ref),
                (agg_hbm, agg_ref),
                (prolong_hbm, prolong_ref),
                (cinv_hbm, cinv_ref),
            ]
        )
    ]
    for load in loads:
        load.start()
    rhs = rhs_ref.at[0, 0]
    parts = 4
    load_blocks = [
        pltpu.make_async_copy(
            blocks_hbm.at[0, 0, pl.ds(p * (nb // parts), nb // parts)],
            blocks.at[pl.ds(p * (nb // parts), nb // parts)],
            load_sem.at[p],
        )
        for p in range(parts)
    ]

    row_up, row_down = (row + 1) % n_row, (row + n_row - 1) % n_row
    col_up, col_down = (col + 1) % n_col, (col + n_col - 1) % n_col
    targets = [(row_up, col), (row_down, col), (row, col_up), (row, col_down)]
    line_a = [((at1 + d) % f1 * f2 + at2, col) for d in range(1, f1)]
    line_b = [(at1 * f2 + (at2 + d) % f2, col) for d in range(1, f2)]
    line_c = [(row, (col + d) % n_col) for d in range(1, n_col)]
    greeted = targets + line_a + line_b + line_c
    barrier = pltpu.get_barrier_semaphore()
    for other in greeted:
        pl.semaphore_signal(barrier, inc=1, device_id=other, device_id_type=MESH)

    loads[0].wait()
    small[...] = jnp.zeros_like(small)
    for i in range(3):
        small[i * 3 : i * 3 + 3, :] = smoother_ref[0, 0, i].astype(f32)
    lanes = iota((16, 9 * vec), 1)
    starts = iota((16, 9 * vec), 0) * vec
    spread = dot_first(
        small[...].astype(bf16), ones_where((lanes >= starts) & (lanes < starts + vec))
    )
    for q in range(9):
        for n in range(nb):
            factors[q, n] = damping * spread[n * gr : (n + 1) * gr, q * vec : (q + 1) * vec]

    def smooth(n, value):
        v = [value[j * gr : (j + 1) * gr] for j in range(3)]
        return jnp.concatenate(
            [
                factors[3 * i, n] * v[0]
                + factors[3 * i + 1, n] * v[1]
                + factors[3 * i + 2, n] * v[2]
                for i in range(3)
            ],
            axis=0,
        )

    def loop(low, high, body, unroll=UNROLL):
        def several(step, carry):
            for u in range(unroll):
                body(low + step * unroll + u)
            return carry

        lax.fori_loop(0, (high - low) // unroll, several, 0)

    def multiply(n, source):
        picked = jnp.concatenate([source[col_ref[0, 0, k, n]] for k in range(kk)], axis=0)
        return dot(blocks[n], picked)

    def halo(packed, source, send_sem, recv_sem):
        return [
            pltpu.make_async_remote_copy(
                src_ref=packed.at[g],
                dst_ref=source.at[pl.ds(nb + g * hb, hb)],
                send_sem=send_sem.at[g],
                recv_sem=recv_sem.at[g],
                device_id=targets[g],
                device_id_type=MESH,
            )
            for g in range(4)
        ]

    def first_body(n):
        value = smooth(n, rhs[n])
        first[n] = value
        source1[n] = value.astype(bf16)

    halo1 = halo(packed1, source1, h1_send, h1_recv)
    for load in loads[1:3]:
        load.wait()
    for load in load_blocks:
        load.start()
    for g in range(4):
        for j in range(hb):
            n = send_ref[0, 0, g, j]
            packed1[g, j] = smooth(n, rhs[n]).astype(bf16)
        if g == 0:
            pl.semaphore_wait(barrier, len(greeted))
        halo1[g].start()
    loop(0, nb, first_body)

    for load in loads[3:]:
        load.wait()
    wide[...] = jnp.zeros_like(wide)
    wide[0:cd, :] = prolong_ref[0, 0].astype(f32)
    rows, modes = iota((32, 8), 0), iota((32, 8), 1)
    hit = rows < 0
    for a in range(agg):
        hit = hit | ((rows == modes + a * cd) & (modes < cd))
    lane = iota((1, nb * dof), 1)
    owner = jnp.zeros((1, nb * dof), jnp.int32)
    for n in range(nb):
        owner = jnp.where(
            (lane >= n * dof) & (lane < (n + 1) * dof), agg_ref[0, 0, n] * cd, owner
        )
    owner = jnp.broadcast_to(owner, (32, nb * dof))
    unknown = iota((32, nb * dof), 0)
    expanded = dot(ones_where(hit), wide[...].astype(bf16))
    pexpt[...] = jnp.where(
        (unknown >= owner) & (unknown < owner + cd), expanded, 0.0
    ).astype(bf16)
    upright = dot_first(pexpt[...], ones_where(iota((32, vec), 0) == iota((32, vec), 1)))
    for n in range(nb):
        source3[n] = upright[n * dof : (n + 1) * dof].astype(bf16)
    modes, origin = iota((32, vec), 0), iota((32, vec), 1)
    for g in range(4):
        total = jnp.zeros((32, dof), f32)
        for j in range(hb):
            n = send_ref[0, 0, g, j]
            hit = modes < 0
            for a in range(agg):
                hit = hit | (origin - a * cd == modes - j * cd)
            hit = hit & (modes >= j * cd) & (modes < (j + 1) * cd) & (origin < cu)
            total = total + lax.dot_general(
                ones_where(hit), source3[n], (((1,), (1,)), ((), ())), preferred_element_type=f32
            )
            shift = (agg_ref[0, 0, n] * cd).astype(f32)
            total = jnp.where(iota((32, dof), 0) == cu + j, shift, total)
        pmsg[g] = total.astype(bf16)

    pmsg_copies = [
        pltpu.make_async_remote_copy(
            src_ref=pmsg.at[g],
            dst_ref=pghost.at[g],
            send_sem=p_send.at[g],
            recv_sem=p_recv.at[g],
            device_id=targets[g],
            device_id_type=MESH,
        )
        for g in range(4)
    ]
    for copy in pmsg_copies:
        copy.start()

    for load in load_blocks:
        load.wait()

    def reduced_body(n):
        value = dot_first(source3[n][:, 0:32], blocks[n])
        high = value.astype(bf16)
        reduced[n, 0:32, :] = high
        reduced[n, 32:64, :] = (value - high.astype(f32)).astype(bf16)

    loop(0, nb, reduced_body)
    cinv32[...] = cinv_ref[...].astype(f32)

    def coarse_rows(c):
        return cinv32[pl.ds(pl.multiple_of(c * cu, 8), cu), :]

    cstack[...] = jnp.zeros_like(cstack)
    cstack[0:cu] = coarse_rows(col)
    cstack[3 * cu : 4 * cu] = coarse_rows(col_down)
    cstack[4 * cu : 5 * cu] = coarse_rows(col_up)
    crow[...] = cstack[0:32].astype(bf16)

    def operator_body(n):
        value = source3[n].astype(f32) - smooth(n, multiply(n, source3))
        high = value.astype(bf16)
        quick[n, :, 0:vec] = high
        quick[n, :, vec : 2 * vec] = (value - high.astype(f32)).astype(bf16)

    half = nb // 2
    for copy in halo1:
        copy.wait_recv()

    def second_body(n):
        value = rhs[n] - multiply(n, source1)
        res[n] = value
        update = smooth(n, value)
        later[n] = first[n] + update
        high = value.astype(bf16)
        place = pl.ds(pl.multiple_of(n * dof, dof), dof)
        residual_low[0, place, :] = high
        residual_low[1, place, :] = (value - high.astype(f32)).astype(bf16)
        source2[n] = update.astype(bf16)
        local[n] = update.astype(bf16)

    halo2 = [
        pltpu.make_async_remote_copy(
            src_ref=packed2.at[g, j],
            dst_ref=source2.at[nb + g * hb + j],
            send_sem=h2_send.at[g * hb + j],
            recv_sem=h2_recv.at[g * hb + j],
            device_id=targets[g],
            device_id_type=MESH,
        )
        for g in range(4)
        for j in range(hb)
    ]
    for j in range(hb):
        for g in range(2):
            n = send_ref[0, 0, g, j]
            packed2[g, j] = smooth(n, rhs[n] - multiply(n, source1)).astype(bf16)
            halo2[g * hb + j].start()
    loop(0, nb, second_body)
    for g in range(2, 4):
        for j in range(hb):
            packed2[g, j] = local[send_ref[0, 0, g, j]]
            halo2[g * hb + j].start()

    before = dot(pexpt[...], residual_low[0]) + dot(pexpt[...], residual_low[1])
    for copy in pmsg_copies:
        copy.wait_recv()
    for g in range(4):
        message = pghost[g]
        wide_message = message.astype(f32)
        for j in range(hb):
            shift = wide_message[cu + j : cu + j + 1, 0:vec]
            column = (origin - (1 + g) * cu - (modes - j * cd)).astype(f32)
            hit = (column == shift) & (modes >= j * cd) & (modes < (j + 1) * cd)
            source3[nb + g * hb + j] = dot_first(message, ones_where(hit)).astype(bf16)

    loop(0, half, operator_body, 3)
    for copy in halo2:
        copy.wait_recv()
    crow_copies = [
        pltpu.make_async_remote_copy(
            src_ref=crow,
            dst_ref=cghost.at[g],
            send_sem=c_send.at[g],
            recv_sem=c_recv.at[g],
            device_id=targets[g],
            device_id_type=MESH,
        )
        for g in range(2)
    ]
    for copy in crow_copies:
        copy.start()

    def take_off(step, total):
        for u in range(UNROLL):
            n = step * UNROLL + u
            picked = jnp.concatenate([source2[col_ref[0, 0, k, n]] for k in range(kk)], axis=0)
            total = total - dot(reduced[n], picked)
        return total

    taken = lax.fori_loop(0, nb // UNROLL, take_off, jnp.zeros((64, vec), f32))
    gathered[at1, at2, col] = (before + (taken[0:32] + taken[32:64])).astype(bf16)

    def step_copies(line, pick, mine, others, send_sem, recv_sem):
        sends, arrivals = [], []
        for d, target in enumerate(line):
            sends.append(
                pltpu.make_async_remote_copy(
                    src_ref=pick(mine),
                    dst_ref=pick(mine),
                    send_sem=send_sem.at[d],
                    recv_sem=recv_sem.at[d],
                    device_id=target,
                    device_id_type=MESH,
                )
            )
            arrivals.append(
                pltpu.make_async_remote_copy(
                    src_ref=pick(mine),
                    dst_ref=pick(others[d]),
                    send_sem=send_sem.at[d],
                    recv_sem=recv_sem.at[d],
                    device_id=target,
                    device_id_type=MESH,
                )
            )
        return sends, arrivals

    def behind(at, count):
        return [(at + count - d) % count for d in range(1, count)]

    a_sends, a_arrivals = step_copies(
        line_a, lambda i: gathered.at[i, at2, col], at1, behind(at1, f1), ga_send, ga_recv
    )
    b_sends, b_arrivals = step_copies(
        line_b, lambda i: gathered.at[:, i, col], at2, behind(at2, f2), gb_send, gb_recv
    )
    c_sends, c_arrivals = step_copies(
        line_c, lambda i: gathered.at[:, :, i], col, behind(col, n_col), gc_send, gc_recv
    )
    for copy in a_sends:
        copy.start()

    def fourth_body(n):
        later[n] = later[n] + smooth(n, res[n] - multiply(n, source2))

    loop(half, half + 3, operator_body, 3)
    write_quick = pltpu.make_async_copy(quick, quick_ref, out_sem.at[1])
    for copy in a_arrivals:
        copy.wait_recv()
    for copy in b_sends:
        copy.start()
    loop(half + 3, nb, operator_body, 3)
    write_quick.start()
    loop(0, 3, fourth_body, 3)
    for copy in b_arrivals:
        copy.wait_recv()
    for copy in c_sends:
        copy.start()
    for copy in crow_copies:
        copy.wait_recv()
    cstack[cu : 2 * cu] = cghost[0].astype(f32)[0:cu]
    cstack[2 * cu : 3 * cu] = cghost[1].astype(f32)[0:cu]
    loop(3, nb, fourth_body, 3)
    write_later = pltpu.make_async_copy(later, later_ref, out_sem.at[0])
    write_later.start()
    cstack_low = cstack[...].astype(bf16)
    for copy in c_arrivals:
        copy.wait_recv()

    def unpad(step, carry):
        for c in range(n_col):
            start = pl.multiple_of((step * n_col + c) * cu, 8)
            grhs[pl.ds(start, cu), :] = gathered[step // f2, step % f2, c].astype(f32)[0:cu]
        return carry

    lax.fori_loop(0, n_row, unpad, 0)
    coarse = dot(cstack_low, grhs[...].astype(bf16)).astype(bf16)
    twice_ref[0:vec, :] = coarse
    twice_ref[vec : 2 * vec, :] = coarse
    for copy in halo1 + crow_copies + halo2 + pmsg_copies + a_sends + b_sends + c_sends:
        copy.wait_send()
    write_later.wait()
    write_quick.wait()


def body(rhs, smoother, blocks, col_index, send_list, agg_id, prolong, coarse_inverse):
    n_row, n_col = lax.axis_size("row"), lax.axis_size("col")
    nb, dof, vec = rhs.shape[2:]
    kk = col_index.shape[3]
    hb = send_list.shape[3]
    cd = prolong.shape[2]
    nc = coarse_inverse.shape[1]
    agg = nc // (n_row * n_col) // cd
    cu = agg * cd
    f2 = 4 if n_row % 4 == 0 else 1
    f1 = n_row // f2
    dims = (n_row, n_col, f1, f2, nb, dof, vec, kk, cd, agg, hb)
    slots = nb + 4 * hb
    field = (nb, dof, vec)
    dma = pltpu.SemaphoreType.DMA
    vmem = pl.BlockSpec(memory_space=pltpu.VMEM)
    anywhere = pl.BlockSpec(memory_space=pl.ANY)
    pinned = pl.BlockSpec(memory_space=pltpu.HBM)
    columns = jnp.swapaxes(col_index, 2, 3)
    later, quick, twice = pl.pallas_call(
        functools.partial(kernel, dims),
        out_shape=[
            jax.ShapeDtypeStruct(field, f32),
            jax.ShapeDtypeStruct((nb, dof, 2 * vec), bf16),
            jax.ShapeDtypeStruct((2 * vec, vec), bf16),
        ],
        in_specs=[pinned] * 8,
        out_specs=[anywhere, anywhere, vmem],
        scratch_shapes=[
            pltpu.VMEM(rhs.shape, f32),
            pltpu.VMEM(smoother.shape, bf16),
            pltpu.SMEM(columns.shape, jnp.int32),
            pltpu.SMEM(send_list.shape, jnp.int32),
            pltpu.SMEM(agg_id.shape, jnp.int32),
            pltpu.VMEM(prolong.shape, bf16),
            pltpu.VMEM(coarse_inverse.shape, bf16),
            pltpu.VMEM(blocks.shape[2:], bf16),
            pltpu.VMEM(field, f32),
            pltpu.VMEM(field, f32),
            pltpu.VMEM(field, f32),
            pltpu.VMEM((9, nb, dof // 3, vec), f32),
            pltpu.VMEM((16, nb * dof // 3), f32),
            pltpu.VMEM((8, nb * dof), f32),
            pltpu.VMEM((slots, dof, vec), bf16),
            pltpu.VMEM((slots, dof, vec), bf16),
            pltpu.VMEM((slots, dof, vec), bf16),
            pltpu.VMEM((4, hb, dof, vec), bf16),
            pltpu.VMEM((4, hb, dof, vec), bf16),
            pltpu.VMEM((4, 32, dof), bf16),
            pltpu.VMEM((4, 32, dof), bf16),
            pltpu.VMEM((n_col * cu, nc), f32),
            pltpu.VMEM((32, nc), bf16),
            pltpu.VMEM((2, 32, nc), bf16),
            pltpu.VMEM((vec, nc), f32),
            pltpu.VMEM((2, nb * dof, vec), bf16),
            pltpu.VMEM((32, nb * dof), bf16),
            pltpu.VMEM((nb, 64, kk * dof), bf16),
            pltpu.VMEM((f1, f2, n_col, 32, vec), bf16),
            pltpu.VMEM((nc, vec), f32),
            pltpu.VMEM((nb, dof, 2 * vec), bf16),
            pltpu.VMEM(field, bf16),
            dma((11,)),
            dma((2,)),
            dma((4,)),
            dma((4,)),
            dma((4 * hb,)),
            dma((4 * hb,)),
            dma((4,)),
            dma((4,)),
            dma((2,)),
            dma((2,)),
            dma((max(f1 - 1, 1),)),
            dma((max(f1 - 1, 1),)),
            dma((max(f2 - 1, 1),)),
            dma((max(f2 - 1, 1),)),
            dma((n_col - 1,)),
            dma((n_col - 1,)),
        ],
        compiler_params=pltpu.CompilerParams(
            collective_id=0, has_side_effects=True, vmem_limit_bytes=57 * 1024 * 1024
        ),
    )(rhs, smoother, blocks, columns, send_list, agg_id, prolong, coarse_inverse)
    return (later + dot(quick, twice))[None, None]


def solution(mesh):
    placed = (
        P("row", "col", None, None, None),
        P("row", "col", None, None, None),
        P("row", "col", None, None, None),
        P("row", "col", None, None),
        P("row", "col", None, None),
        P("row", "col", None),
        P("row", "col", None, None),
        P("row", None),
    )
    return jax.shard_map(
        body,
        mesh=mesh,
        in_specs=placed,
        out_specs=P("row", "col", None, None, None),
        check_vma=False,
    )
```
